32 devices in a mesh: dp: 4 (over z), expert: 2 (over y), context: 4 (over x, core).
Axes of the slice: x: 2, y: 2, z: 4, core: 2. Of those that a mesh axis runs over, the one named last changes fastest.
Arguments:
- inputs: bfloat16 [32, 512, 512], P(('dp', 'expert'), 'context'), may hold values from -6 to 6
- cotangent: bfloat16 [32, 512, 512], P(('dp', 'expert'), 'context'), may hold values from -6 to 6
- routes: int32 [4, 32, 128, 2], P('context', ('dp', 'expert')), may hold values from 0 to 31, all different within a row; in each aligned block of 256 rows (0 to 255, 256 to 511, ..., all dimensions but the last counted through in order) at most 32 rows name the same one
- gates: float32 [4, 32, 128, 2], P('context', ('dp', 'expert')), may hold values from 0.3 to 0.7
- attn_gain: bfloat16 [512], P('dp'), may hold values from 0.099609375 to 1.8984375
- attn_shift: bfloat16 [512], P('dp'), may hold values from -0.59765625 to 0.59765625
- qkv_weight: bfloat16 [512, 1536], P('dp'), may hold values from -0.25 to 0.25
- query_bias: bfloat16 [512], P('dp'), may hold values from -0.59765625 to 0.59765625
- value_bias: bfloat16 [512], P('dp'), may hold values from -0.119628906 to 0.119628906
- proj_weight: bfloat16 [512, 512], P('dp'), may hold values from -2 to 2
- proj_bias: bfloat16 [512], P('dp'), may hold values from -0.59765625 to 0.59765625
- mlp_gain: bfloat16 [512], P('dp'), may hold values from 0.099609375 to 1.8984375
- mlp_shift: bfloat16 [512], P('dp'), may hold values from -0.59765625 to 0.59765625
- expert_in: bfloat16 [32, 512, 2048], P('expert'), may hold values from -0.25 to 0.25
- expert_in_bias: bfloat16 [32, 2048], P('expert'), may hold values from -0.59765625 to 0.59765625
- expert_out: bfloat16 [32, 2048, 512], P('expert'), may hold values from -0.1875 to 0.1875
- expert_out_bias: bfloat16 [32, 512], P('expert'), may hold values from -0.59765625 to 0.59765625
Outputs:
- result: bfloat16 [32, 512, 512], P(('dp', 'expert'), 'context')
- input_grad: float32 [32, 512, 512], P(('dp', 'expert'), 'context')
- gate_grad: float32 [4, 32, 128, 2], P('context', ('dp', 'expert'))
- attn_gain_grad: float32 [512], P('dp')
- attn_shift_grad: float32 [512], P('dp')
- qkv_weight_grad: float32 [512, 1536], P('dp')
- query_bias_grad: float32 [512], P('dp')
- value_bias_grad: float32 [512], P('dp')
- proj_weight_grad: float32 [512, 512], P('dp')
- proj_bias_grad: float32 [512], P('dp')
- mlp_gain_grad: float32 [512], P('dp')
- mlp_shift_grad: float32 [512], P('dp')
- expert_in_grad: float32 [32, 512, 2048], P('expert', None, ('dp', 'context'))
- expert_in_bias_grad: float32 [32, 2048], P('expert', ('dp', 'context'))
- expert_out_grad: float32 [32, 2048, 512], P('expert', ('dp', 'context'))
- expert_out_bias_grad: float32 [32, 512], P('expert', ('dp', 'context'))
The draws below stay inside these ranges and needn't reach their ends.
Inputs may be any that keep to these rules, and one draw needn't show every extreme that they name: `routes`: each row names 2 different experts. In each aligned block of 256 rows (leading dimensions in order: the tokens of 2 images at one place along the context dimension) no expert is named more than 32 times, and in some blocks one is named exactly 32 times.
All inputs are finite; a program needn't handle non-finite values.
Results may differ from the reference program's by a relative error of at most 0.02.
Values may be sent and summed in bfloat16 or wider, within the bound.
No kernel may reach another device: no remote copies, remote signals or barrier semaphores. Data moves between devices by JAX's collectives and lax.ppermute only.
A program may use at most 384 MiB of HBM per device.

```python
import math
import jax
import jax.numpy as jnp
import numpy as np
from jax import lax

D = 512
H = 2048
HEADS = 8
EXPERTS = 32
HEAD_DIM = 64
TOP = 2
CTX_TOK = 128
IMG_MB = 2
IMAGES = 32
SEQ = 512
TOK_MB = 256
CAP = 32
N_CONTEXT = 4


def block_levels(own_key, extent, shards, low, largest):
    def one(dim, shards_of):
        draws = jax.random.uniform(jax.random.fold_in(jax.random.fold_in(own_key, 6), dim), (shards_of,), jnp.float32, low / len(shards), largest / len(shards))
        return jnp.repeat(jnp.exp(draws), extent[dim] // shards_of).reshape((-1,) + (1,) * (len(extent) - dim - 1))

    gain = one(*shards[0])
    for cut in shards[1:]:
        gain = gain * one(*cut)
    return gain


def routed_block(rng, own, number, rows, amount, top, limit, lean):
    sequence = jax.random.permutation(rng, amount)
    crowded, usual = shares(amount, rows * top, limit, lean, True), shares(amount, rows * top, limit, lean, False)
    places = jnp.arange(amount)

    def named(tallies, turn):
        used = int((tallies > 0).sum())
        fixed = max(1, used // 4)
        moved = fixed + (places - fixed + turn * (used - fixed)) % max(1, amount - fixed)
        return jnp.zeros((amount,), jnp.int32).at[sequence[jnp.where(places < fixed, places, moved)]].set(jnp.asarray(tallies, jnp.int32))

    tallies = jnp.where(number % 4 == 0, named(crowded, number // 4), named(usual, number - number // 4 - 1))
    mixed = jax.random.permutation(jax.random.fold_in(own, 3), amount)
    giver, taker = mixed[0:amount // 2 * 2:2], mixed[1:amount // 2 * 2:2]
    margin = jnp.minimum(tallies[giver] - 1, limit - tallies[taker]) // 2
    margin = jnp.where((giver == sequence[0]) | (taker == sequence[0]) | (tallies[taker] == 0), 0, jnp.maximum(margin, 0))
    moved = jax.random.randint(jax.random.fold_in(own, 4), (amount // 2,), 0, 1 << 20) % (margin + 1)
    tallies = tallies.at[giver].add(-moved).at[taker].add(moved)
    labels = jnp.searchsorted(jnp.cumsum(tallies), jnp.arange(rows * top), side="right").astype(jnp.int32)
    table = labels.reshape(top, rows).T
    table = table[jax.random.permutation(jax.random.fold_in(own, 1), rows)]
    turn = jax.random.randint(jax.random.fold_in(own, 2), (rows, 1), 0, top)
    return jnp.take_along_axis(table, (jnp.arange(top)[None, :] + turn) % top, axis=1)


def shares(count, total, limit, lean, full):
    loads = [(1 << 20) // math.isqrt(rank ** lean) + 1 for rank in range(1, count + 1)]
    largest = limit if full else min(limit, max(-(-total // count), total * loads[0] // sum(loads)))
    least = 1 if total - largest >= count - 1 else 0
    holding, spare = [largest] + [least] * (count - 1), total - largest - least * (count - 1)
    while spare > 0:
        free = [i for i in range(1, count) if holding[i] < largest] or [i for i in range(1, count) if holding[i] < limit]
        mass, remaining = sum([loads[i] for i in free]), spare
        for i in free:
            extra = min(limit - holding[i], max(1, remaining * loads[i] // mass), spare)
            holding[i] = holding[i] + extra
            spare = spare - extra
    return np.array(holding)


def gaussian(own_key, extent, scale, reach, cuts=(), kind=jnp.bfloat16):
    drawn = jax.random.normal(own_key, extent, jnp.float32) * scale
    if len(cuts) > 0:
        drawn = block_levels(own_key, extent, cuts, -0.22, 0.18) * drawn
    return jnp.clip(drawn, min=-reach, max=reach).astype(kind)


def setup_inputs(seed: int = 0) -> dict:
    keys = jax.random.split(jax.random.key(seed), 18)
    inputs = gaussian(keys[0], (IMAGES, SEQ, D), 1.0, 6.0, ((0, 8), (1, 4)))
    cotangent = gaussian(keys[1], (IMAGES, SEQ, D), 1.0, 6.0, ((0, 8), (1, 4)))
    routes_keys = jax.random.split(jax.random.fold_in(keys[2], 1), N_CONTEXT * IMAGES * CTX_TOK // TOK_MB)
    routes_turns = jax.random.permutation(jax.random.fold_in(keys[2], 3), N_CONTEXT * IMAGES * CTX_TOK // TOK_MB)
    routes = jax.vmap(lambda own, number: routed_block(jax.random.fold_in(keys[2], 2), own, number, TOK_MB, EXPERTS, TOP, CAP, 1))(routes_keys, routes_turns).reshape((N_CONTEXT, IMAGES, CTX_TOK, TOP))
    gates = jnp.clip(0.3 + 0.39999998 * jax.random.uniform(keys[3], (N_CONTEXT, IMAGES, CTX_TOK, TOP), jnp.float32) ** block_levels(keys[3], (N_CONTEXT, IMAGES, CTX_TOK, TOP), ((0, 4), (1, 8)), -0.2, 0.2), 0.3, 0.7)
    attn_gain = jnp.clip(1.0 + 0.18 * jax.random.normal(keys[4], (D,), jnp.float32), 0.099609375, 1.8984375).astype(jnp.bfloat16)
    attn_shift = gaussian(keys[5], (D,), 0.1, 0.59765625, ((0, 4),))
    qkv_weight = gaussian(keys[6], (D, 3 * D), D ** -0.5, 0.25, ((0, 4),))
    query_bias = gaussian(keys[7], (D,), 0.1, 0.59765625, ((0, 4),))
    value_bias = gaussian(keys[8], (D,), 0.02, 0.119628906, ((0, 4),))
    proj_weight = gaussian(keys[9], (D, D), (max(1, D // 64)) ** -0.5, 2.0, ((0, 4),))
    proj_bias = gaussian(keys[10], (D,), 0.1, 0.59765625, ((0, 4),))
    mlp_gain = jnp.clip(1.0 + 0.18 * jax.random.normal(keys[11], (D,), jnp.float32), 0.099609375, 1.8984375).astype(jnp.bfloat16)
    mlp_shift = gaussian(keys[12], (D,), 0.1, 0.59765625, ((0, 4),))
    expert_in = gaussian(keys[13], (EXPERTS, D, H), D ** -0.5, 0.25, ((0, 2),))
    expert_in_bias = gaussian(keys[14], (EXPERTS, H), 0.1, 0.59765625, ((0, 2),))
    expert_out = gaussian(keys[15], (EXPERTS, H, D), (H // 2) ** -0.5, 0.1875, ((0, 2),))
    expert_out_bias = gaussian(keys[16], (EXPERTS, D), 0.1, 0.59765625, ((0, 2),))
    return {"inputs": inputs, "cotangent": cotangent, "routes": routes, "gates": gates, "attn_gain": attn_gain, "attn_shift": attn_shift, "qkv_weight": qkv_weight, "query_bias": query_bias, "value_bias": value_bias, "proj_weight": proj_weight, "proj_bias": proj_bias, "mlp_gain": mlp_gain, "mlp_shift": mlp_shift, "expert_in": expert_in, "expert_in_bias": expert_in_bias, "expert_out": expert_out, "expert_out_bias": expert_out_bias}


EPSILON = 1e-06
HIGHEST = lax.Precision.HIGHEST

@jax.custom_vjp
def low(v):
    return lax.optimization_barrier(v.astype(jnp.bfloat16)).astype(jnp.float32)

@jax.custom_vjp
def low_back(v):
    return v

def low_keep(v):
    return (low(v), None)

def low_pass(kept, grad):
    return (grad,)

def back_keep(v):
    return (v, None)

def back_low(kept, grad):
    return (low(grad),)
low.defvjp(low_keep, low_pass)
low_back.defvjp(back_keep, back_low)

def layer_norm(values, gain_vec, shift_vec):
    average = lax.optimization_barrier(jnp.mean(values, axis=-1, keepdims=True))
    centred = values - average
    spread = lax.optimization_barrier(jnp.mean(centred * centred, axis=-1, keepdims=True))
    return centred * lax.rsqrt(spread + EPSILON) * gain_vec + shift_vec

def gelu_exact(values):
    return 0.5 * values * (1.0 + jax.scipy.special.erf(values * (1.0 / math.sqrt(2.0))))

def slot_places(route_rows):
    flat = route_rows.reshape(-1)
    table = (flat[:, None] == jnp.arange(EXPERTS, dtype=jnp.int32)[None, :]).astype(jnp.int32)
    earlier = jnp.cumsum(table, axis=0) - table
    return lax.optimization_barrier(jnp.sum(earlier * table, axis=1)).astype(jnp.int32)

def forward(weight_set, block_x, block_gates, block_routes, slot_ids):
    attn_gain, attn_shift, qkv_weight, query_bias, value_bias, proj_weight, proj_bias, mlp_gain, mlp_shift, expert_in, expert_in_bias, expert_out, expert_out_bias = weight_set
    images = block_x.shape[0]
    normed = low(layer_norm(block_x, attn_gain, attn_shift))
    joined = jnp.einsum('bsd,de->bse', normed, qkv_weight, precision=HIGHEST)
    queries = low_back(low(joined[..., :D] + query_bias)).reshape(images, SEQ, HEADS, HEAD_DIM)
    key_rows = low_back(low(joined[..., D:2 * D])).reshape(images, SEQ, HEADS, HEAD_DIM)
    value_rows = low_back(low(joined[..., 2 * D:] + value_bias)).reshape(images, SEQ, HEADS, HEAD_DIM)
    scores = low_back(jnp.einsum('bqhd,bkhd->bhqk', queries, key_rows, precision=HIGHEST) * (1.0 / math.sqrt(HEAD_DIM)))
    highest = lax.optimization_barrier(jnp.max(scores, axis=-1, keepdims=True))
    exponent = jnp.exp(scores - highest)
    probabilities = low(exponent / lax.optimization_barrier(jnp.sum(exponent, axis=-1, keepdims=True)))
    attended = jnp.einsum('bhqk,bkhd->bqhd', probabilities, value_rows, precision=HIGHEST)
    attended = low_back(low(attended)).reshape(images, SEQ, D)
    branch = low_back(jnp.einsum('bsd,de->bse', attended, proj_weight, precision=HIGHEST) + proj_bias)
    middle = block_x + branch
    second = low(layer_norm(middle, mlp_gain, mlp_shift))
    arranged = second.reshape(images, N_CONTEXT, CTX_TOK, D).transpose(1, 0, 2, 3)
    blocks = jnp.broadcast_to(jnp.arange(N_CONTEXT, dtype=jnp.int32)[:, None, None, None], block_routes.shape)
    copies = jnp.broadcast_to(arranged[:, :, :, None, :], block_routes.shape + (D,))
    buffer = jnp.zeros((N_CONTEXT, EXPERTS, CAP, D), block_x.dtype).at[blocks, block_routes, slot_ids].add(copies)
    buffer = low_back(buffer)
    pre_act = low_back(jnp.einsum('cerd,edh->cerh', buffer, expert_in, precision=HIGHEST) + expert_in_bias[None, :, None, :])
    hidden = low(gelu_exact(pre_act))
    produced = jnp.einsum('cerh,ehd->cerd', hidden, expert_out, precision=HIGHEST) + expert_out_bias[None, :, None, :]
    produced = low_back(low(produced))
    picked = produced[blocks, block_routes, slot_ids]
    combined = lax.optimization_barrier(jnp.sum(picked * block_gates[..., None], axis=3))
    combined = combined.transpose(1, 0, 2, 3).reshape(images, SEQ, D)
    return middle + combined

def reference(inputs, cotangent, routes, gates, attn_gain, attn_shift, qkv_weight, query_bias, value_bias, proj_weight, proj_bias, mlp_gain, mlp_shift, expert_in, expert_in_bias, expert_out, expert_out_bias):
    weights = tuple((weight_arg.astype(jnp.float32) for weight_arg in (attn_gain, attn_shift, qkv_weight, query_bias, value_bias, proj_weight, proj_bias, mlp_gain, mlp_shift, expert_in, expert_in_bias, expert_out, expert_out_bias)))
    steps_count = IMAGES // IMG_MB
    inputs_steps = inputs.astype(jnp.float32).reshape(steps_count, IMG_MB, SEQ, D)
    cot_steps = cotangent.astype(jnp.float32).reshape(steps_count, IMG_MB, SEQ, D)
    routes_steps = routes.reshape(N_CONTEXT, steps_count, IMG_MB, CTX_TOK, TOP).transpose(1, 0, 2, 3, 4)
    gates_steps = gates.astype(jnp.float32).reshape(N_CONTEXT, steps_count, IMG_MB, CTX_TOK, TOP).transpose(1, 0, 2, 3, 4)

    def one_step(totals, pieces):
        block_in, block_cot, block_routes, block_gates = pieces
        slot_ids = jax.vmap(slot_places)(block_routes.reshape(N_CONTEXT, -1, TOP)).reshape(block_routes.shape)

        def wrapped(weight_set, block_x, block_g):
            return forward(weight_set, block_x, block_g, block_routes, slot_ids)
        output, pullback = jax.vjp(wrapped, weights, block_in, block_gates)
        weight_grads, input_grads, gate_grads = pullback(block_cot)
        return (jax.tree.map(jnp.add, totals, weight_grads), (output, input_grads, gate_grads))
    zeros_set = jax.tree.map(jnp.zeros_like, weights)
    totals, (outputs, input_grads, gate_grads) = lax.scan(one_step, zeros_set, (inputs_steps, cot_steps, routes_steps, gates_steps))
    gate_grad = gate_grads.transpose(1, 0, 2, 3, 4).reshape(N_CONTEXT, IMAGES, CTX_TOK, TOP)
    return (outputs.reshape(IMAGES, SEQ, D).astype(jnp.bfloat16), input_grads.reshape(IMAGES, SEQ, D), gate_grad, totals[0], totals[1], totals[2], totals[3], totals[4], totals[5], totals[6], totals[7], totals[8], totals[9], totals[10], totals[11], totals[12])
```

```python
import functools
import math

import jax
import jax.numpy as jnp
from jax import lax
from jax.experimental import pallas as pl
from jax.experimental.pallas import tpu as pltpu
from jax.sharding import PartitionSpec as P

EXPERTS = 32
HEAD_DIM = 64
TOP = 2
CAP = 32

EPSILON = 1e-06
ROOT_HALF = 1.0 / math.sqrt(2.0)
INV_ROOT_TWO_PI = 1.0 / math.sqrt(2.0 * math.pi)
SCORE_SCALE = 1.0 / math.sqrt(HEAD_DIM)

F32 = jnp.float32
BF16 = jnp.bfloat16
VMEM_LIMIT = 56 * 1024 * 1024

GAIN_ONE, SHIFT_ONE, QUERY_BIAS, VALUE_BIAS, PROJ_BIAS, GAIN_TWO, SHIFT_TWO = range(7)

NN = (((1,), (0,)), ((), ()))
NT = (((1,), (1,)), ((), ()))
TN = (((0,), (0,)), ((), ()))


def mul(a, b, how=NN):
    return lax.dot_general(a, b, how, preferred_element_type=F32)


def norm_stats(values):
    average = jnp.mean(values, axis=-1, keepdims=True)
    centred = values - average
    inverse = lax.rsqrt(jnp.mean(centred * centred, axis=-1, keepdims=True) + EPSILON)
    return centred * inverse, inverse


def norm_back(scaled, inverse, gain_vec, grad_out):
    grad_scaled = grad_out * gain_vec
    mean_grad = jnp.mean(grad_scaled, axis=-1, keepdims=True)
    mean_cross = jnp.mean(grad_scaled * scaled, axis=-1, keepdims=True)
    return inverse * (grad_scaled - mean_grad - scaled * mean_cross)


def gelu_parts(values):
    spread = jnp.abs(values) * ROOT_HALF
    t = 1.0 / (1.0 + 0.3275911 * spread)
    series = t * (
        0.254829592
        + t * (-0.284496736 + t * (1.421413741 + t * (-1.453152027 + t * 1.061405429)))
    )
    bell = jnp.exp(-0.5 * values * values)
    tail = 0.5 * series * bell
    return jnp.where(values >= 0.0, 1.0 - tail, tail), bell * INV_ROOT_TWO_PI


def attn_fwd_kernel(
    x_ref, wqkv_ref, wproj_ref, vec_ref, qkv_ref, probs_ref, att_ref, mid_ref, sec_ref
):
    width = x_ref.shape[1]
    pairs = width // (2 * HEAD_DIM)
    x = x_ref[...].astype(F32)
    scaled, _ = norm_stats(x)
    vec = vec_ref[...]
    normed = (scaled * vec[GAIN_ONE : GAIN_ONE + 1] + vec[SHIFT_ONE : SHIFT_ONE + 1]).astype(BF16)
    queries = mul(normed, wqkv_ref[:, :width]) + vec[QUERY_BIAS : QUERY_BIAS + 1]
    qkv_ref[:, :width] = (queries.astype(BF16).astype(F32) * SCORE_SCALE).astype(BF16)
    qkv_ref[:, width : 2 * width] = mul(normed, wqkv_ref[:, width : 2 * width]).astype(BF16)
    qkv_ref[:, 2 * width :] = (
        mul(normed, wqkv_ref[:, 2 * width :]) + vec[VALUE_BIAS : VALUE_BIAS + 1]
    ).astype(BF16)
    rows = lax.broadcasted_iota(jnp.int32, (2 * HEAD_DIM, 1), 0)
    for pair in range(pairs):
        at = pair * 2 * HEAD_DIM
        query_t = qkv_ref[:, at : at + 2 * HEAD_DIM].astype(F32).T
        keys = qkv_ref[:, width + at : width + at + 2 * HEAD_DIM]
        value_t = qkv_ref[:, 2 * width + at : 2 * width + at + 2 * HEAD_DIM].astype(F32).T.astype(BF16)
        outs = []
        for half in range(2):
            own = (rows // HEAD_DIM) == half
            scores = mul(keys, jnp.where(own, query_t, 0.0).astype(BF16))
            highest = jnp.max(scores, axis=0, keepdims=True)
            exponent = jnp.exp(scores - highest)
            total = jnp.sum(exponent, axis=0, keepdims=True)
            probs = (exponent * (1.0 / total)).astype(BF16)
            probs_ref[2 * pair + half] = probs
            outs.append(mul(value_t[half * HEAD_DIM : (half + 1) * HEAD_DIM], probs))
        att_ref[:, at : at + 2 * HEAD_DIM] = jnp.concatenate(outs, axis=0).T.astype(BF16)
    middle = x + mul(att_ref[...], wproj_ref[...]) + vec[PROJ_BIAS : PROJ_BIAS + 1]
    mid_ref[...] = middle
    scaled_two, _ = norm_stats(middle)
    sec_ref[...] = (
        scaled_two * vec[GAIN_TWO : GAIN_TWO + 1] + vec[SHIFT_TWO : SHIFT_TWO + 1]
    ).astype(BF16)


def attn_fwd(x, wqkv, wproj, vec):
    rows, width = x.shape
    heads = width // HEAD_DIM
    return pl.pallas_call(
        attn_fwd_kernel,
        out_shape=(
            jax.ShapeDtypeStruct((rows, 3 * width), BF16),
            jax.ShapeDtypeStruct((heads, rows, rows), BF16),
            jax.ShapeDtypeStruct((rows, width), BF16),
            jax.ShapeDtypeStruct((rows, width), F32),
            jax.ShapeDtypeStruct((rows, width), BF16),
        ),
        compiler_params=pltpu.CompilerParams(vmem_limit_bytes=VMEM_LIMIT),
        cost_estimate=pl.CostEstimate(
            flops=8 * rows * width * width + 4 * rows * rows * width * 2,
            bytes_accessed=12 * rows * width + 8 * width * width + 2 * heads * rows * rows,
            transcendentals=heads * rows * rows,
        ),
        name="attn_fwd",
    )(x, wqkv, wproj, vec)


def attn_bwd_kernel(
    gs_ref, cot_ref, mid_ref, att_ref, qkv_ref, probs_ref, x_ref, wqkv_ref, wproj_ref, vec_ref,
    ig_ref, dw_ref, dvec_ref, gj_ref,
):
    width = x_ref.shape[1]
    pairs = width // (2 * HEAD_DIM)
    vec = vec_ref[...]
    grad_second = gs_ref[...].astype(F32)
    scaled_two, inverse_two = norm_stats(mid_ref[...])
    grad_middle = cot_ref[...].astype(F32) + norm_back(
        scaled_two, inverse_two, vec[GAIN_TWO : GAIN_TWO + 1], grad_second
    )
    dvec_ref[GAIN_TWO : GAIN_TWO + 1] = jnp.sum(grad_second * scaled_two, axis=0, keepdims=True)
    dvec_ref[SHIFT_TWO : SHIFT_TWO + 1] = jnp.sum(grad_second, axis=0, keepdims=True)
    grad_branch = grad_middle.astype(BF16)
    dvec_ref[PROJ_BIAS : PROJ_BIAS + 1] = jnp.sum(grad_branch.astype(F32), axis=0, keepdims=True)
    dw_ref[:, 3 * width :] = mul(att_ref[...], grad_branch, TN).astype(BF16)
    grad_att = mul(grad_branch, wproj_ref[...], NT).astype(BF16)
    rows = lax.broadcasted_iota(jnp.int32, (2 * HEAD_DIM, 1), 0)
    lanes = lax.broadcasted_iota(jnp.int32, (1, 2 * HEAD_DIM), 1)
    for pair in range(pairs):
        at = pair * 2 * HEAD_DIM
        grad_heads = grad_att[:, at : at + 2 * HEAD_DIM]
        grad_t = grad_heads.astype(F32).T
        queries = qkv_ref[:, at : at + 2 * HEAD_DIM]
        key_t = qkv_ref[:, width + at : width + at + 2 * HEAD_DIM].astype(F32).T.astype(BF16)
        values = qkv_ref[:, 2 * width + at : 2 * width + at + 2 * HEAD_DIM]
        query_t, key_sides, value_sides = [], [], []
        for half in range(2):
            own = (rows // HEAD_DIM) == half
            low = probs_ref[2 * pair + half]
            probs = low.astype(F32)
            grad_probs = mul(values, jnp.where(own, grad_t, 0.0).astype(BF16))
            inner = jnp.sum(probs * grad_probs, axis=0, keepdims=True)
            grad_scores = (probs * (grad_probs - inner)).astype(BF16)
            value_sides.append(mul(low, grad_heads))
            key_sides.append(mul(grad_scores, queries))
            query_t.append(mul(key_t[half * HEAD_DIM : (half + 1) * HEAD_DIM], grad_scores))
        first = lanes < HEAD_DIM
        gj_ref[:, at : at + 2 * HEAD_DIM] = (
            jnp.concatenate(query_t, axis=0).T * SCORE_SCALE
        ).astype(BF16)
        gj_ref[:, width + at : width + at + 2 * HEAD_DIM] = jnp.where(
            first, key_sides[0], key_sides[1]
        ).astype(BF16)
        gj_ref[:, 2 * width + at : 2 * width + at + 2 * HEAD_DIM] = jnp.where(
            first, value_sides[0], value_sides[1]
        ).astype(BF16)
    dvec_ref[QUERY_BIAS : QUERY_BIAS + 1] = jnp.sum(
        gj_ref[:, :width].astype(F32), axis=0, keepdims=True
    )
    dvec_ref[VALUE_BIAS : VALUE_BIAS + 1] = jnp.sum(
        gj_ref[:, 2 * width :].astype(F32), axis=0, keepdims=True
    )
    scaled_one, inverse_one = norm_stats(x_ref[...].astype(F32))
    normed = (
        scaled_one * vec[GAIN_ONE : GAIN_ONE + 1] + vec[SHIFT_ONE : SHIFT_ONE + 1]
    ).astype(BF16)
    for part in range(3):
        at = part * width
        dw_ref[:, at : at + width] = mul(normed, gj_ref[:, at : at + width], TN).astype(BF16)
    grad_normed = mul(gj_ref[...], wqkv_ref[...], NT)
    dvec_ref[GAIN_ONE : GAIN_ONE + 1] = jnp.sum(grad_normed * scaled_one, axis=0, keepdims=True)
    dvec_ref[SHIFT_ONE : SHIFT_ONE + 1] = jnp.sum(grad_normed, axis=0, keepdims=True)
    dvec_ref[7:8] = jnp.zeros((1, width), F32)
    ig_ref[...] = (
        grad_middle
        + norm_back(scaled_one, inverse_one, vec[GAIN_ONE : GAIN_ONE + 1], grad_normed)
    ).astype(BF16)


def attn_bwd(gs, cot, mid, att, qkv, probs, x, wqkv, wproj, vec):
    rows, width = x.shape
    heads = width // HEAD_DIM
    return pl.pallas_call(
        attn_bwd_kernel,
        out_shape=(
            jax.ShapeDtypeStruct((rows, width), BF16),
            jax.ShapeDtypeStruct((width, 4 * width), BF16),
            jax.ShapeDtypeStruct((8, width), F32),
        ),
        scratch_shapes=[pltpu.VMEM((rows, 3 * width), BF16)],
        compiler_params=pltpu.CompilerParams(vmem_limit_bytes=VMEM_LIMIT),
        cost_estimate=pl.CostEstimate(
            flops=16 * rows * width * width + 8 * rows * rows * width * 2,
            bytes_accessed=20 * rows * width + 16 * width * width + 2 * heads * rows * rows,
            transcendentals=0,
        ),
        name="attn_bwd",
    )(gs, cot, mid, att, qkv, probs, x, wqkv, wproj, vec)


def expert_kernel(parts, pref_ref, *refs):
    toks = refs[:parts]
    cots = refs[parts : 2 * parts]
    mrow_ref, win_ref, wout_ref, bin_ref, bout_ref = refs[2 * parts : 2 * parts + 5]
    outs = refs[2 * parts + 5 :]
    results = outs[:parts]
    seconds = outs[parts : 2 * parts]
    gate_ref, xo_ref, go_ref, ao_ref, po_ref, x_scr, g_scr, y_scr, d_scr = outs[2 * parts :]
    step = pl.program_id(0)
    count, _, width = x_scr.shape
    slots = count * CAP
    half = toks[0].shape[2]
    first_code = pref_ref[0]

    @pl.when(step == 0)
    def _():
        place = (lax.broadcasted_iota(jnp.int32, (slots, 2 * half), 0) + first_code).astype(F32)
        for part in range(parts):
            for block in range(2):
                meta = mrow_ref[pref_ref[2 + part], block]
                zero = place == meta[0:1]
                one = place == meta[1:2]
                pick = jnp.where(zero | one, 1.0, 0.0).astype(BF16)
                gated = jnp.where(zero, meta[2:3], jnp.where(one, meta[3:4], 0.0)).astype(BF16)
                rows = jnp.concatenate([toks[part][0, block], toks[part][1, block]], axis=0)
                cot = jnp.concatenate([cots[part][0, block], cots[part][1, block]], axis=0)
                at = (2 * part + block) * CAP
                x_scr[:, at : at + CAP, :] = mul(pick, rows).astype(BF16).reshape(count, CAP, width)
                g_scr[:, at : at + CAP, :] = mul(gated, cot).astype(BF16).reshape(count, CAP, width)

    x = x_scr[step]
    g = g_scr[step]
    xo_ref[0] = x
    go_ref[0] = g
    pre_act = mul(x, win_ref[0]) + bin_ref[0]
    grad_active = mul(g, wout_ref[0], NT)
    below, density = gelu_parts(pre_act)
    active = (pre_act * below).astype(BF16)
    grad_pre = (grad_active * (below + pre_act * density)).astype(BF16)
    ao_ref[0] = active
    po_ref[0] = grad_pre
    bias = jnp.where(pref_ref[1] == 0, bout_ref[0], 0.0)
    y_scr[step] = (mul(active, wout_ref[0]) + bias).astype(BF16)
    d_scr[step] = mul(grad_pre, win_ref[0], NT).astype(BF16)

    @pl.when(step == count - 1)
    def _():
        place = (lax.broadcasted_iota(jnp.int32, (2 * half, slots), 1) + first_code).astype(F32)
        for part in range(parts):
            for block in range(2):
                meta = mrow_ref[pref_ref[2 + part], block].T
                at = (2 * part + block) * CAP
                zero = jnp.where(place == meta[:, 0:1], 1.0, 0.0)
                one = jnp.where(place == meta[:, 1:2], 1.0, 0.0)
                produced = y_scr[:, at : at + CAP, :].reshape(slots, width)
                grads = d_scr[:, at : at + CAP, :].reshape(slots, width)
                cot = jnp.concatenate([cots[part][0, block], cots[part][1, block]], axis=0).astype(F32)
                picked_zero = mul(zero.astype(BF16), produced)
                picked_one = mul(one.astype(BF16), produced)
                gate_ref[part, block, :, 0:1] = jnp.sum(picked_zero * cot, axis=1, keepdims=True)
                gate_ref[part, block, :, 1:2] = jnp.sum(picked_one * cot, axis=1, keepdims=True)
                combined = (picked_zero * meta[:, 2:3] + picked_one * meta[:, 3:4]).astype(BF16)
                results[part][0, block] = combined[:half]
                results[part][1, block] = combined[half:]
                second = mul((zero + one).astype(BF16), grads).astype(BF16)
                seconds[part][0, block] = second[:half]
                seconds[part][1, block] = second[half:]


def expert_pass(pref, toks, cots, mrow, win, wout, bin_, bout):
    parts = len(toks)
    count, width, hidden = win.shape
    rows = parts * 2 * CAP
    shape = toks[0].shape
    whole = lambda a: pl.BlockSpec(a.shape, lambda e, s, n=len(a.shape): (0,) * n)
    each = lambda *s: pl.BlockSpec((1,) + s, lambda e, p: (e, 0, 0))
    gate_shape = (parts, 2, 2 * shape[2], TOP)
    tok_struct = jax.ShapeDtypeStruct(shape, BF16)
    return pl.pallas_call(
        functools.partial(expert_kernel, parts),
        grid_spec=pltpu.PrefetchScalarGridSpec(
            num_scalar_prefetch=1,
            grid=(count,),
            in_specs=[whole(t) for t in toks]
            + [whole(c) for c in cots]
            + [
                whole(mrow),
                each(width, hidden),
                each(hidden, width),
                each(1, hidden),
                each(1, width),
            ],
            out_specs=[whole(t) for t in toks]
            + [whole(t) for t in toks]
            + [
                pl.BlockSpec(gate_shape, lambda e, p: (0, 0, 0, 0)),
                each(rows, width),
                each(rows, width),
                each(rows, hidden),
                each(rows, hidden),
            ],
            scratch_shapes=[pltpu.VMEM((count, rows, width), BF16)] * 4,
        ),
        out_shape=[tok_struct] * (2 * parts)
        + [
            jax.ShapeDtypeStruct(gate_shape, F32),
            jax.ShapeDtypeStruct((count, rows, width), BF16),
            jax.ShapeDtypeStruct((count, rows, width), BF16),
            jax.ShapeDtypeStruct((count, rows, hidden), BF16),
            jax.ShapeDtypeStruct((count, rows, hidden), BF16),
        ],
        compiler_params=pltpu.CompilerParams(
            vmem_limit_bytes=VMEM_LIMIT, dimension_semantics=("arbitrary",)
        ),
        cost_estimate=pl.CostEstimate(
            flops=16 * count * rows * width * hidden,
            bytes_accessed=4 * count * width * hidden + 8 * count * rows * (width + hidden),
            transcendentals=2 * count * rows * hidden,
        ),
        name="expert_pass",
    )(pref, *toks, *cots, mrow, win, wout, bin_, bout)


def expert_grad_kernel(groups, *refs):
    xs = refs[:groups]
    gs = refs[groups : 2 * groups]
    acts = refs[2 * groups : 3 * groups]
    pres = refs[3 * groups : 4 * groups]
    in_ref, out_ref, inb_ref, outb_ref = refs[4 * groups :]
    total_in = total_out = bias_in = bias_out = None
    for i in range(groups):
        x, g, a, p = xs[i][0], gs[i][0], acts[i][0], pres[i][0]
        d_in, d_out = mul(x, p, TN), mul(a, g, TN)
        b_in = jnp.sum(p.astype(F32), axis=0, keepdims=True)
        b_out = jnp.sum(g.astype(F32), axis=0, keepdims=True)
        if i == 0:
            total_in, total_out, bias_in, bias_out = d_in, d_out, b_in, b_out
        else:
            total_in, total_out = total_in + d_in, total_out + d_out
            bias_in, bias_out = bias_in + b_in, bias_out + b_out
    cut = in_ref.shape[3]
    for place in range(in_ref.shape[0]):
        at = place * cut
        in_ref[place, 0] = total_in[:, at : at + cut].astype(BF16)
        out_ref[place, 0] = total_out[at : at + cut].astype(BF16)
    inb_ref[0] = bias_in
    outb_ref[0] = bias_out


def expert_grads(xs, gs, acts, pres, cuts):
    groups = len(xs)
    count, _, width = xs[0].shape
    hidden = acts[0].shape[2]
    each = lambda a: pl.BlockSpec((1,) + a.shape[1:], lambda e: (e, 0, 0))
    rows = sum(x.shape[1] for x in xs)
    return pl.pallas_call(
        functools.partial(expert_grad_kernel, groups),
        grid=(count,),
        in_specs=[each(a) for a in (*xs, *gs, *acts, *pres)],
        out_specs=[
            pl.BlockSpec((cuts, 1, width, hidden // cuts), lambda e: (0, e, 0, 0)),
            pl.BlockSpec((cuts, 1, hidden // cuts, width), lambda e: (0, e, 0, 0)),
            pl.BlockSpec((1, 1, hidden), lambda e: (e, 0, 0)),
            pl.BlockSpec((1, 1, width), lambda e: (e, 0, 0)),
        ],
        out_shape=[
            jax.ShapeDtypeStruct((cuts, count, width, hidden // cuts), BF16),
            jax.ShapeDtypeStruct((cuts, count, hidden // cuts, width), BF16),
            jax.ShapeDtypeStruct((count, 1, hidden), F32),
            jax.ShapeDtypeStruct((count, 1, width), F32),
        ],
        compiler_params=pltpu.CompilerParams(
            vmem_limit_bytes=VMEM_LIMIT, dimension_semantics=("arbitrary",)
        ),
        cost_estimate=pl.CostEstimate(
            flops=4 * count * rows * width * hidden,
            bytes_accessed=4 * count * (rows + width) * (width + hidden),
            transcendentals=0,
        ),
        name="expert_grads",
    )(*xs, *gs, *acts, *pres)


def pick_row(array, index):
    return lax.dynamic_index_in_dim(array, index, 0, keepdims=False)


def local(
    inputs,
    cotangent,
    routes,
    gates,
    attn_gain,
    attn_shift,
    qkv_weight,
    query_bias,
    value_bias,
    proj_weight,
    proj_bias,
    mlp_gain,
    mlp_shift,
    expert_in,
    expert_in_bias,
    expert_out,
    expert_out_bias,
):
    n_dp, n_expert, n_ctx = (lax.axis_size(a) for a in ("dp", "expert", "context"))
    z, y, c = (lax.axis_index(a) for a in ("dp", "expert", "context"))
    images, tok, width = inputs.shape
    count = expert_in.shape[0]
    hidden = expert_in.shape[2] // n_dp
    cut = hidden // n_ctx

    def near(a):
        return lax.ppermute(a, "context", [(i, i ^ 1) for i in range(n_ctx)])

    def far(a):
        return lax.ppermute(a, "context", [(i, i ^ 2) for i in range(n_ctx)])

    def along(a, axis, n, by):
        return lax.ppermute(a, axis, [(i, (i + by) % n) for i in range(n)])

    def xor_order(a):
        return jnp.stack([pick_row(a, c ^ m) for m in range(images)])

    def to_blocks(a):
        turned = xor_order(a)
        got = far(turned[2:])
        return jnp.stack([turned[:2], got], axis=1)

    x_blocks = to_blocks(inputs)
    small = to_blocks(
        jnp.concatenate([routes[0].astype(F32), gates[0]], axis=-1).transpose(0, 2, 1)
    )
    x_image = jnp.concatenate([x_blocks[0], near(x_blocks[1])], axis=0).reshape(-1, width)

    low = c & 1
    pack = jnp.concatenate([qkv_weight, proj_weight], axis=1)
    half_rows = pack.shape[0] // 2
    current = lax.dynamic_slice_in_dim(pack, low * half_rows, half_rows, 0)
    held = [current]
    for _ in range(n_dp - 1):
        current = along(current, "dp", n_dp, 1)
        held.append(current)
    other = [near(a) for a in held]
    held = jnp.stack(held)
    other = jnp.stack(other)
    rows = []
    for i in range(n_dp):
        at = (z - i) % n_dp
        one, two = pick_row(held, at), pick_row(other, at)
        rows += [jnp.where(low == 0, one, two), jnp.where(low == 0, two, one)]
    weights = jnp.concatenate(rows, axis=0)
    wqkv, wproj = weights[:, : 3 * width], weights[:, 3 * width :]
    vectors = jnp.stack(
        [attn_gain, attn_shift, query_bias, value_bias, proj_bias, mlp_gain, mlp_shift, mlp_shift]
    )
    vec = lax.all_gather(vectors, "dp", axis=1, tiled=True).astype(F32)

    entries = small[:, :, :TOP].transpose(1, 0, 3, 2).reshape(2, -1)
    table = (entries[:, :, None] == jnp.arange(EXPERTS, dtype=F32)[None, None, :]).astype(BF16)
    order = jnp.arange(entries.shape[1])
    lower = (order[:, None] > order[None, :]).astype(BF16)
    earlier = jnp.einsum("ij,bje->bie", lower, table, preferred_element_type=F32)
    slot_ids = jnp.sum(earlier * table.astype(F32), axis=2)
    codes = (entries * CAP + slot_ids).reshape(2, 2 * tok, TOP).transpose(0, 2, 1)
    gate_rows = small[:, :, TOP:].transpose(1, 2, 0, 3).reshape(2, TOP, 2 * tok)
    meta = jnp.concatenate([codes, gate_rows, codes, gate_rows], axis=1)
    mrow = lax.all_gather(meta, ("dp", "expert"), axis=0, tiled=False)

    turns = (0, 2, 1, 3)
    firsts = [(z * n_ctx + (c ^ t)) * cut for t in turns]
    win = jnp.concatenate(
        [lax.dynamic_slice_in_dim(expert_in, f, cut, 2) for f in firsts], axis=2
    )
    wout = jnp.concatenate(
        [lax.dynamic_slice_in_dim(expert_out, f, cut, 1) for f in firsts], axis=1
    )
    bin_ = jnp.concatenate(
        [lax.dynamic_slice_in_dim(expert_in_bias, f, cut, 1) for f in firsts], axis=1
    ).astype(F32)[:, None, :]
    bout = expert_out_bias.astype(F32)[:, None, :]

    def spread(own):
        current, all_parts = own, []
        for k in range(n_dp):
            all_parts.append(
                [current] + [along(current, "expert", n_expert, -j) for j in range(1, n_expert)]
            )
            if k < n_dp - 1:
                current = along(current, "dp", n_dp, 1)
        return all_parts

    cot_blocks = to_blocks(cotangent)
    cot_parts = spread(cot_blocks)
    cot_image = jnp.concatenate([cot_blocks[0], near(cot_blocks[1])], axis=0).reshape(-1, width)

    qkv, probs, attended, middle, second = attn_fwd(x_image, wqkv, wproj, vec)

    second = second.reshape(2, 2, tok, width)
    second_blocks = jnp.stack([second[0], near(second[1])])
    mid_side = middle.reshape(2, 2, tok, width)
    mid_blocks = jnp.stack([mid_side[0], near(mid_side[1].astype(BF16)).astype(F32)])
    tok_parts = spread(second_blocks)

    groups = [[k] for k in range(n_dp)]
    result_parts, second_parts, gate_parts = [], [], []
    kept = [[], [], [], []]
    for group in groups:
        toks = [t for k in group for t in tok_parts[k]]
        cots = [t for k in group for t in cot_parts[k]]
        sources = [
            ((z - k) % n_dp) * n_expert + (y + j) % n_expert for k in group for j in range(n_expert)
        ]
        pref = jnp.stack([y * (count * CAP), z] + sources).astype(jnp.int32)
        outs = expert_pass(pref, toks, cots, mrow, win, wout, bin_, bout)
        parts = len(toks)
        for i in range(len(group)):
            result_parts.append(outs[i * n_expert : (i + 1) * n_expert])
            second_parts.append(outs[parts + i * n_expert : parts + (i + 1) * n_expert])
            gate_parts.append(outs[2 * parts][i * n_expert : (i + 1) * n_expert])
        for keep, out in zip(kept, outs[2 * parts + 1 :]):
            keep.append(out)

    grads_in, grads_out, bias_in, bias_out = expert_grads(*kept, n_ctx)

    def collect(parts):
        travelling = None
        for k in list(range(1, n_dp)) + [0]:
            total = parts[k][0].astype(F32)
            for j in range(1, n_expert):
                total = total + along(parts[k][j], "expert", n_expert, j).astype(F32)
            if travelling is not None:
                total = total + travelling.astype(F32)
            if k != 0:
                travelling = along(total.astype(parts[k][0].dtype), "dp", n_dp, 1)
        return total

    grad_second = collect(second_parts)
    gs_low = grad_second.astype(BF16)
    gs_image = jnp.concatenate([gs_low[0], near(gs_low[1])], axis=0).reshape(-1, width)
    ig, dw, dvec = attn_bwd(
        gs_image, cot_image, middle, attended, qkv, probs, x_image, wqkv, wproj, vec
    )

    def from_blocks(a):
        got = far(a[:, 1])
        return xor_order(jnp.concatenate([a[:, 0], got], axis=0))

    combined = collect(result_parts)
    result = from_blocks((combined + mid_blocks).astype(BF16))

    gate_sum = collect(gate_parts)
    gate_sum = gate_sum.reshape(2, 2, tok, TOP).transpose(1, 0, 2, 3)
    gate_grad = from_blocks(gate_sum)[None]

    ig = ig.reshape(2, 2, tok, width)
    input_grad = from_blocks(jnp.stack([ig[0], near(ig[1])])).astype(F32)

    def halve(a):
        got = near(a[2:])
        send = (a[1].astype(F32) + got[1].astype(F32)).astype(a.dtype)
        return a[0].astype(F32) + got[0].astype(F32) + far(send).astype(F32)

    in_grad = halve(grads_in)
    out_grad = halve(grads_out)
    in_bias_grad = halve(bias_in.reshape(count, n_ctx, cut).transpose(1, 0, 2))
    bias_out = bias_out[:, 0]
    bias_out = bias_out + near(bias_out)
    bias_out = bias_out + far(bias_out)
    share = width // (n_dp * n_ctx)
    out_bias_grad = lax.dynamic_slice_in_dim(bias_out, (z * n_ctx + c) * share, share, 1)

    def halve_rows(a, bit, swap):
        n = a.shape[1] // 2
        keep = lax.dynamic_slice_in_dim(a, bit * n, n, 1)
        send = lax.dynamic_slice_in_dim(a, (1 - bit) * n, n, 1)
        return (keep.astype(F32) + swap(send).astype(F32)).astype(a.dtype)

    def double_rows(a, bit, swap):
        got = swap(a)
        return jnp.concatenate([jnp.where(bit == 0, a, got), jnp.where(bit == 0, got, a)], axis=0)

    def all_expert(a):
        total = a.astype(F32)
        for j in range(1, n_expert):
            total = total + along(a, "expert", n_expert, j).astype(F32)
        return total.astype(a.dtype)

    def over_dp(a):
        total = pick_row(a, z).astype(F32)
        for k in range(1, n_dp):
            total = total + along(pick_row(a, (z + k) % n_dp), "dp", n_dp, k).astype(F32)
        return total

    high = c >> 1
    dw = dw.reshape(n_dp, width // n_dp, 4 * width)
    dw = halve_rows(dw, low, near)
    dw = halve_rows(dw, high, far)
    if n_expert == 2:
        dw = halve_rows(dw, y, lambda a: along(a, "expert", n_expert, 1))
    else:
        dw = all_expert(dw)
    dw = over_dp(dw).astype(BF16)
    if n_expert == 2:
        dw = double_rows(dw, y, lambda a: along(a, "expert", n_expert, 1))
    dw = double_rows(dw, high, far)
    dw = double_rows(dw, low, near).astype(F32)

    dvec = dvec + near(dvec)
    dvec = dvec + far(dvec)
    dvec = all_expert(dvec)
    dvec = over_dp(dvec.reshape(8, n_dp, -1).transpose(1, 0, 2))

    return (
        result,
        input_grad,
        gate_grad,
        dvec[GAIN_ONE],
        dvec[SHIFT_ONE],
        dw[:, : 3 * width],
        dvec[QUERY_BIAS],
        dvec[VALUE_BIAS],
        dw[:, 3 * width :],
        dvec[PROJ_BIAS],
        dvec[GAIN_TWO],
        dvec[SHIFT_TWO],
        in_grad,
        in_bias_grad,
        out_grad,
        out_bias_grad,
    )


def solution(mesh):
    return jax.shard_map(
        local,
        mesh=mesh,
        in_specs=(
            P(("dp", "expert"), "context", None),
            P(("dp", "expert"), "context", None),
            P("context", ("dp", "expert"), None, None),
            P("context", ("dp", "expert"), None, None),
            P("dp"),
            P("dp"),
            P("dp", None),
            P("dp"),
            P("dp"),
            P("dp", None),
            P("dp"),
            P("dp"),
            P("dp"),
            P("expert", None, None),
            P("expert", None),
            P("expert", None, None),
            P("expert", None),
        ),
        out_specs=(
            P(("dp", "expert"), "context", None),
            P(("dp", "expert"), "context", None),
            P("context", ("dp", "expert"), None, None),
            P("dp"),
            P("dp"),
            P("dp", None),
            P("dp"),
            P("dp"),
            P("dp", None),
            P("dp"),
            P("dp"),
            P("dp"),
            P("expert", None, ("dp", "context")),
            P("expert", ("dp", "context")),
            P("expert", ("dp", "context"), None),
            P("expert", ("dp", "context")),
        ),
        check_vma=False,
    )
```

```python
import functools
import math

import jax
import jax.numpy as jnp
from jax import lax
from jax.experimental import pallas as pl
from jax.experimental.pallas import tpu as pltpu
from jax.sharding import PartitionSpec as P

EXPERTS = 32
HEAD_DIM = 64
TOP = 2
CAP = 32

EPSILON = 1e-06
ROOT_HALF = 1.0 / math.sqrt(2.0)
INV_ROOT_TWO_PI = 1.0 / math.sqrt(2.0 * math.pi)
SCORE_SCALE = 1.0 / math.sqrt(HEAD_DIM)

F32 = jnp.float32
BF16 = jnp.bfloat16
VMEM_LIMIT = 56 * 1024 * 1024


def cost(microseconds):
    return pl.CostEstimate(flops=int(microseconds * 1e9), bytes_accessed=1, transcendentals=0)


GAIN_ONE, SHIFT_ONE, QUERY_BIAS, VALUE_BIAS, PROJ_BIAS, GAIN_TWO, SHIFT_TWO = range(7)

NN = (((1,), (0,)), ((), ()))
NT = (((1,), (1,)), ((), ()))
TN = (((0,), (0,)), ((), ()))


def mul(a, b, how=NN):
    return lax.dot_general(a, b, how, preferred_element_type=F32)


def norm_stats(values):
    average = jnp.mean(values, axis=-1, keepdims=True)
    centred = values - average
    inverse = lax.rsqrt(jnp.mean(centred * centred, axis=-1, keepdims=True) + EPSILON)
    return centred * inverse, inverse


def norm_back(scaled, inverse, gain_vec, grad_out):
    grad_scaled = grad_out * gain_vec
    mean_grad = jnp.mean(grad_scaled, axis=-1, keepdims=True)
    mean_cross = jnp.mean(grad_scaled * scaled, axis=-1, keepdims=True)
    return inverse * (grad_scaled - mean_grad - scaled * mean_cross)


def gelu_parts(values):
    spread = jnp.abs(values) * ROOT_HALF
    t = 1.0 / (1.0 + 0.3275911 * spread)
    series = t * (
        0.254829592
        + t * (-0.284496736 + t * (1.421413741 + t * (-1.453152027 + t * 1.061405429)))
    )
    bell = jnp.exp(-0.5 * values * values)
    tail = 0.5 * series * bell
    return jnp.where(values >= 0.0, 1.0 - tail, tail), bell * INV_ROOT_TWO_PI


def skipping(deps, kernel, *refs):
    kernel(*refs[deps:])


def call_after(deps, kernel, in_specs, **options):
    deps = list(deps)
    call = pl.pallas_call(
        functools.partial(skipping, len(deps), kernel),
        in_specs=[pl.BlockSpec(memory_space=pl.ANY)] * len(deps) + list(in_specs),
        compiler_params=pltpu.CompilerParams(vmem_limit_bytes=VMEM_LIMIT),
        **options,
    )
    return lambda *arrays: call(*deps, *arrays)


def after(arrays, *deps):
    token = lax.optimization_barrier((lax.create_token(), *deps))[0]
    return [lax.optimization_barrier((token, a))[1] for a in arrays]


def attn_fwd_kernel(
    n_dp, place_ref, own_ref, far_ref, near_ref, qkv_own_ref, proj_own_ref, vec_own_ref, other_ref,
    *refs,
):
    got = refs[: n_dp - 1]
    (
        qkv_ref, probs_ref, att_ref, mid_ref, keep_ref, send_ref, x_ref, wqkv_ref, wproj_ref, vec_ref,
        vec_scr,
    ) = refs[n_dp - 1 :]
    rows, width = x_ref.shape
    quarter = rows // 4
    x_ref[:quarter] = own_ref[...]
    x_ref[quarter : 2 * quarter] = far_ref[...]
    x_ref[2 * quarter : 3 * quarter] = near_ref[0]
    x_ref[3 * quarter :] = near_ref[1]
    z, low = place_ref[0], place_ref[1]
    part_rows = width // n_dp
    half_rows = part_rows // 2

    def put(at, block):
        at = pl.ds(pl.multiple_of(at, half_rows), block.shape[0])
        wqkv_ref[at] = block[:, : 3 * width]
        wproj_ref[at] = block[:, 3 * width :]

    at = pl.ds(pl.multiple_of(z * part_rows, part_rows), part_rows)
    wqkv_ref[at] = qkv_own_ref[...]
    wproj_ref[at] = proj_own_ref[...]
    vec_scr[z] = vec_own_ref[...].astype(F32)
    for k in range(1, n_dp):
        source = lax.rem(z + n_dp - k, n_dp)
        put(source * part_rows + low * half_rows, got[k - 1][:half_rows])
        put(source * part_rows + (1 - low) * half_rows, other_ref[k - 1, :half_rows])
        vec_scr[source] = got[k - 1][half_rows : half_rows + 16, :part_rows].astype(F32)[:8]
    vec_ref[...] = jnp.concatenate([vec_scr[k] for k in range(n_dp)], axis=1)
    pairs = width // (2 * HEAD_DIM)
    x = x_ref[...].astype(F32)
    scaled, _ = norm_stats(x)
    vec = vec_ref[...]
    normed = (scaled * vec[GAIN_ONE : GAIN_ONE + 1] + vec[SHIFT_ONE : SHIFT_ONE + 1]).astype(BF16)
    queries = mul(normed, wqkv_ref[:, :width]) + vec[QUERY_BIAS : QUERY_BIAS + 1]
    qkv_ref[:, :width] = (queries.astype(BF16).astype(F32) * SCORE_SCALE).astype(BF16)
    qkv_ref[:, width : 2 * width] = mul(normed, wqkv_ref[:, width : 2 * width]).astype(BF16)
    qkv_ref[:, 2 * width :] = (
        mul(normed, wqkv_ref[:, 2 * width :]) + vec[VALUE_BIAS : VALUE_BIAS + 1]
    ).astype(BF16)
    head_rows = lax.broadcasted_iota(jnp.int32, (2 * HEAD_DIM, 1), 0)
    for pair in range(pairs):
        at = pair * 2 * HEAD_DIM
        query_t = qkv_ref[:, at : at + 2 * HEAD_DIM].astype(F32).T
        keys = qkv_ref[:, width + at : width + at + 2 * HEAD_DIM]
        value_t = qkv_ref[:, 2 * width + at : 2 * width + at + 2 * HEAD_DIM].astype(F32).T.astype(BF16)
        outs = []
        for half in range(2):
            own = (head_rows // HEAD_DIM) == half
            scores = mul(keys, jnp.where(own, query_t, 0.0).astype(BF16))
            highest = jnp.max(scores, axis=0, keepdims=True)
            exponent = jnp.exp(scores - highest)
            total = jnp.sum(exponent, axis=0, keepdims=True)
            probs = (exponent * (1.0 / total)).astype(BF16)
            probs_ref[2 * pair + half] = probs
            outs.append(mul(value_t[half * HEAD_DIM : (half + 1) * HEAD_DIM], probs))
        att_ref[:, at : at + 2 * HEAD_DIM] = jnp.concatenate(outs, axis=0).T.astype(BF16)
    middle = x + mul(att_ref[...], wproj_ref[...]) + vec[PROJ_BIAS : PROJ_BIAS + 1]
    mid_ref[...] = middle
    scaled_two, _ = norm_stats(middle)
    second = (
        scaled_two * vec[GAIN_TWO : GAIN_TWO + 1] + vec[SHIFT_TWO : SHIFT_TWO + 1]
    ).astype(BF16)
    keep_ref[...] = second[: rows // 2]
    send_ref[...] = second[rows // 2 :]


def attn_fwd(deps, place, own, far, near, qkv_own, proj_own, vec_own, other, got):
    rows, width = 4 * own.shape[0], own.shape[1]
    heads = width // HEAD_DIM
    n_dp = len(got) + 1
    vmem = pl.BlockSpec(memory_space=pltpu.VMEM)
    return call_after(
        deps,
        functools.partial(attn_fwd_kernel, n_dp),
        in_specs=[pl.BlockSpec(memory_space=pltpu.SMEM)] + [vmem] * (7 + len(got)),
        out_specs=[vmem] * 10,
        out_shape=(
            jax.ShapeDtypeStruct((rows, 3 * width), BF16),
            jax.ShapeDtypeStruct((heads, rows, rows), BF16),
            jax.ShapeDtypeStruct((rows, width), BF16),
            jax.ShapeDtypeStruct((rows, width), F32),
            jax.ShapeDtypeStruct((rows // 2, width), BF16),
            jax.ShapeDtypeStruct((rows // 2, width), BF16),
            jax.ShapeDtypeStruct((rows, width), BF16),
            jax.ShapeDtypeStruct((width, 3 * width), BF16),
            jax.ShapeDtypeStruct((width, width), BF16),
            jax.ShapeDtypeStruct((8, width), F32),
        ),
        scratch_shapes=[pltpu.VMEM((n_dp, 8, width // n_dp), F32)],
        cost_estimate=cost(11),
        name="attn_fwd",
    )(place, own, far, near, qkv_own, proj_own, vec_own, other, *got)


def attn_bwd_kernel(
    gs_keep_ref, gs_near_ref, cot_ref, mid_ref, att_ref, qkv_ref, probs_ref, x_ref, wqkv_ref, wproj_ref, vec_ref,
    ig_keep_ref, ig_send_ref, dw_ref, gj_ref, dvec_ref,
):
    width = x_ref.shape[1]
    pairs = width // (2 * HEAD_DIM)
    dvec_ref[...] = jnp.zeros_like(dvec_ref)
    vec = vec_ref[...]
    grad_second = jnp.concatenate([gs_keep_ref[...], gs_near_ref[...]], axis=0).astype(F32)
    scaled_two, inverse_two = norm_stats(mid_ref[...])
    grad_middle = cot_ref[...].astype(F32) + norm_back(
        scaled_two, inverse_two, vec[GAIN_TWO : GAIN_TWO + 1], grad_second
    )
    dvec_ref[GAIN_TWO : GAIN_TWO + 1] = jnp.sum(grad_second * scaled_two, axis=0, keepdims=True)
    dvec_ref[SHIFT_TWO : SHIFT_TWO + 1] = jnp.sum(grad_second, axis=0, keepdims=True)
    grad_branch = grad_middle.astype(BF16)
    dvec_ref[PROJ_BIAS : PROJ_BIAS + 1] = jnp.sum(grad_branch.astype(F32), axis=0, keepdims=True)
    dw_ref[:, 3 * width : 4 * width] = mul(att_ref[...], grad_branch, TN).astype(BF16)
    grad_att = mul(grad_branch, wproj_ref[...], NT).astype(BF16)
    rows = lax.broadcasted_iota(jnp.int32, (2 * HEAD_DIM, 1), 0)
    lanes = lax.broadcasted_iota(jnp.int32, (1, 2 * HEAD_DIM), 1)
    for pair in range(pairs):
        at = pair * 2 * HEAD_DIM
        grad_heads = grad_att[:, at : at + 2 * HEAD_DIM]
        grad_t = grad_heads.astype(F32).T
        queries = qkv_ref[:, at : at + 2 * HEAD_DIM]
        key_t = qkv_ref[:, width + at : width + at + 2 * HEAD_DIM].astype(F32).T.astype(BF16)
        values = qkv_ref[:, 2 * width + at : 2 * width + at + 2 * HEAD_DIM]
        query_t, key_sides, value_sides = [], [], []
        for half in range(2):
            own = (rows // HEAD_DIM) == half
            low = probs_ref[2 * pair + half]
            probs = low.astype(F32)
            grad_probs = mul(values, jnp.where(own, grad_t, 0.0).astype(BF16))
            inner = jnp.sum(probs * grad_probs, axis=0, keepdims=True)
            grad_scores = (probs * (grad_probs - inner)).astype(BF16)
            value_sides.append(mul(low, grad_heads))
            key_sides.append(mul(grad_scores, queries))
            query_t.append(mul(key_t[half * HEAD_DIM : (half + 1) * HEAD_DIM], grad_scores))
        first = lanes < HEAD_DIM
        gj_ref[:, at : at + 2 * HEAD_DIM] = (
            jnp.concatenate(query_t, axis=0).T * SCORE_SCALE
        ).astype(BF16)
        gj_ref[:, width + at : width + at + 2 * HEAD_DIM] = jnp.where(
            first, key_sides[0], key_sides[1]
        ).astype(BF16)
        gj_ref[:, 2 * width + at : 2 * width + at + 2 * HEAD_DIM] = jnp.where(
            first, value_sides[0], value_sides[1]
        ).astype(BF16)
    dvec_ref[QUERY_BIAS : QUERY_BIAS + 1] = jnp.sum(
        gj_ref[:, :width].astype(F32), axis=0, keepdims=True
    )
    dvec_ref[VALUE_BIAS : VALUE_BIAS + 1] = jnp.sum(
        gj_ref[:, 2 * width :].astype(F32), axis=0, keepdims=True
    )
    scaled_one, inverse_one = norm_stats(x_ref[...].astype(F32))
    normed = (
        scaled_one * vec[GAIN_ONE : GAIN_ONE + 1] + vec[SHIFT_ONE : SHIFT_ONE + 1]
    ).astype(BF16)
    for part in range(3):
        at = part * width
        dw_ref[:, at : at + width] = mul(normed, gj_ref[:, at : at + width], TN).astype(BF16)
    grad_normed = mul(gj_ref[...], wqkv_ref[...], NT)
    dvec_ref[GAIN_ONE : GAIN_ONE + 1] = jnp.sum(grad_normed * scaled_one, axis=0, keepdims=True)
    dvec_ref[SHIFT_ONE : SHIFT_ONE + 1] = jnp.sum(grad_normed, axis=0, keepdims=True)
    dw_ref[:, 4 * width :] = dvec_ref[...].T.astype(BF16)
    grad_input = (
        grad_middle
        + norm_back(scaled_one, inverse_one, vec[GAIN_ONE : GAIN_ONE + 1], grad_normed)
    ).astype(BF16)
    side = grad_input.shape[0] // 2
    ig_keep_ref[...] = grad_input[:side]
    ig_send_ref[...] = grad_input[side:]


def attn_bwd(deps, gs_keep, gs_near, cot, mid, att, qkv, probs, x, wqkv, wproj, vec):
    rows, width = x.shape
    vmem = pl.BlockSpec(memory_space=pltpu.VMEM)
    return call_after(
        deps,
        attn_bwd_kernel,
        in_specs=[vmem] * 11,
        out_specs=[vmem] * 3,
        out_shape=(
            jax.ShapeDtypeStruct((rows // 2, width), BF16),
            jax.ShapeDtypeStruct((rows // 2, width), BF16),
            jax.ShapeDtypeStruct((width, 4 * width + 128), BF16),
        ),
        scratch_shapes=[pltpu.VMEM((rows, 3 * width), BF16), pltpu.VMEM((128, width), F32)],
        cost_estimate=cost(14),
        name="attn_bwd",
    )(gs_keep, gs_near, cot, mid, att, qkv, probs, x, wqkv, wproj, vec)


def block_meta(cot_ref, block):
    half = cot_ref.shape[1] // 2
    at = cot_ref.shape[0] - META_ROWS
    rows = cot_ref[at : at + META_ROWS].astype(F32)[4 * block : 4 * block + 4]
    return jnp.concatenate([rows[:, :half], rows[:, half:]], axis=0)


def block_rows(ref, block):
    quarter = (ref.shape[0] - ref.shape[0] % 64) // 4
    first = ref[block * quarter : (block + 1) * quarter]
    return jnp.concatenate([first, ref[(2 + block) * quarter : (3 + block) * quarter]], axis=0)


def expert_kernel(parts, others, pref_ref, *refs):
    toks = refs[:parts]
    cots = refs[parts : 2 * parts]
    win_ref, wout_ref, bin_ref, bout_ref = refs[2 * parts : 2 * parts + 4]
    outs = refs[2 * parts + 4 :]
    seconds = outs[:parts]
    steps = parts // (others + 1)
    outs = outs[parts:]
    results = []
    for i in range(steps):
        results.append(outs[i])
        for j in range(others):
            high = outs[i].shape[0]
            results.append(outs[steps + j].at[i * high : (i + 1) * high])
    outs = outs[steps + others :]
    xo_ref, go_ref, ao_ref, po_ref = outs[:4]
    x_scr, g_scr, a_scr, p_scr, y_scr, d_scr, in_buf, out_buf, in_sem, out_sem, keep_sem = outs[4:]
    count, _, width = x_scr.shape
    slots = count * CAP
    half = toks[0].shape[0] // 4
    first_code = pref_ref[0].astype(F32)
    depth, _, hidden = in_buf.shape
    part_at = pl.ds(pl.multiple_of(pref_ref[1] * hidden, hidden), hidden)

    def fetch(e, slot):
        return (
            pltpu.make_async_copy(win_ref.at[e, :, part_at], in_buf.at[slot], in_sem.at[slot]),
            pltpu.make_async_copy(wout_ref.at[e, part_at], out_buf.at[slot], out_sem.at[slot]),
        )

    for e in range(min(depth, count)):
        for copy in fetch(e, e):
            copy.start()

    place = lax.broadcasted_iota(jnp.int32, (slots, 2 * half), 0).astype(F32)
    for part in range(parts):
        for block in range(2):
            meta = block_meta(cots[part], block)
            codes = [meta[k : k + 1] * CAP + meta[2 + k : 3 + k] - first_code for k in range(2)]
            zero = place == codes[0]
            one = place == codes[1]
            pick = jnp.where(zero | one, 1.0, 0.0).astype(BF16)
            gated = jnp.where(zero, meta[4:5], jnp.where(one, meta[5:6], 0.0)).astype(BF16)
            at = (2 * part + block) * CAP
            x_scr[:, at : at + CAP, :] = (
                mul(pick, block_rows(toks[part], block)).astype(BF16).reshape(count, CAP, width)
            )
            g_scr[:, at : at + CAP, :] = (
                mul(gated, block_rows(cots[part], block)).astype(BF16).reshape(count, CAP, width)
            )

    def keep(e, i):
        source = (x_scr, g_scr, a_scr, p_scr)[i]
        target = (xo_ref, go_ref, ao_ref, po_ref)[i]
        return pltpu.make_async_copy(source.at[e], target.at[e], keep_sem.at[i, e])

    def one_expert(e, carry):
        slot = lax.rem(e, depth)
        for copy in fetch(e, slot):
            copy.wait()
        x = x_scr[e]
        g = g_scr[e]
        pre_act = mul(x, in_buf[slot]) + bin_ref[e]
        grad_active = mul(g, out_buf[slot], NT)
        below, density = gelu_parts(pre_act)
        active = (pre_act * below).astype(BF16)
        grad_pre = (grad_active * (below + pre_act * density)).astype(BF16)
        a_scr[e] = active
        p_scr[e] = grad_pre
        bias = jnp.where(pref_ref[1] == 0, bout_ref[e], 0.0)
        y_scr[e] = (mul(active, out_buf[slot]) + bias).astype(BF16)
        d_scr[e] = mul(grad_pre, in_buf[slot], NT).astype(BF16)
        for i in range(4):
            keep(e, i).start()

        @pl.when(e + depth < count)
        def _():
            for copy in fetch(e + depth, slot):
                copy.start()

        return carry

    lax.fori_loop(0, count, one_expert, 0)

    place = lax.broadcasted_iota(jnp.int32, (2 * half, slots), 1).astype(F32)
    for part in range(parts):
        gate_sums = []
        for block in range(2):
            meta = block_meta(cots[part], block).T
            codes = [meta[:, k : k + 1] * CAP + meta[:, 2 + k : 3 + k] - first_code for k in range(2)]
            at = (2 * part + block) * CAP
            zero = jnp.where(place == codes[0], 1.0, 0.0)
            one = jnp.where(place == codes[1], 1.0, 0.0)
            produced = y_scr[:, at : at + CAP, :].reshape(slots, width)
            grads = d_scr[:, at : at + CAP, :].reshape(slots, width)
            second = mul((zero + one).astype(BF16), grads).astype(BF16)
            seconds[part][block * half : (block + 1) * half] = second[:half]
            seconds[part][(2 + block) * half : (3 + block) * half] = second[half:]
            cot = block_rows(cots[part], block).astype(F32)
            picked_zero = mul(zero.astype(BF16), produced)
            picked_one = mul(one.astype(BF16), produced)
            gates = [meta[:, 4 + k : 5 + k] + meta[:, 6 + k : 7 + k] for k in range(2)]
            combined = (picked_zero * gates[0] + picked_one * gates[1]).astype(BF16)
            results[part][block * half : (block + 1) * half] = combined[:half]
            results[part][(2 + block) * half : (3 + block) * half] = combined[half:]
            sums = [jnp.sum(p * cot, axis=1, keepdims=True) for p in (picked_zero, picked_one)]
            sums = jnp.concatenate(sums + [jnp.zeros((2 * half, 6), F32)], axis=1).T
            gate_sums.append(jnp.concatenate([sums, jnp.zeros_like(sums)], axis=1))
        results[part][4 * half :] = jnp.concatenate(gate_sums, axis=0).astype(BF16)

    def settle(e, carry):
        for i in range(4):
            keep(e, i).wait()
        return carry

    lax.fori_loop(0, count, settle, 0)


META_ROWS = 16


def expert_pass(deps, others, pref, toks, cots, win, wout, bin_, bout):
    parts = len(toks)
    count, width = win.shape[:2]
    hidden = bin_.shape[2]
    rows = parts * 2 * CAP
    steps = parts // (others + 1)
    vmem = pl.BlockSpec(memory_space=pltpu.VMEM)
    hbm = pl.BlockSpec(memory_space=pl.ANY)
    depth = min(3, count)
    return call_after(
        deps,
        functools.partial(expert_kernel, parts, others),
        in_specs=[pl.BlockSpec(memory_space=pltpu.SMEM)] + [vmem] * (2 * parts) + [hbm, hbm, vmem, vmem],
        out_specs=[vmem] * (parts + steps + others) + [hbm] * 4,
        scratch_shapes=[pltpu.VMEM((count, rows, width), BF16)] * 2
        + [pltpu.VMEM((count, rows, hidden), BF16)] * 2
        + [pltpu.VMEM((count, rows, width), BF16)] * 2
        + [
            pltpu.VMEM((depth, width, hidden), BF16),
            pltpu.VMEM((depth, hidden, width), BF16),
            pltpu.SemaphoreType.DMA((depth,)),
            pltpu.SemaphoreType.DMA((depth,)),
            pltpu.SemaphoreType.DMA((4, count)),
        ],
        out_shape=[jax.ShapeDtypeStruct(toks[0].shape, BF16)] * parts
        + [jax.ShapeDtypeStruct(cots[0].shape, BF16)] * steps
        + [jax.ShapeDtypeStruct((steps * cots[0].shape[0], width), BF16)] * others
        + [
            jax.ShapeDtypeStruct((count, rows, width), BF16),
            jax.ShapeDtypeStruct((count, rows, width), BF16),
            jax.ShapeDtypeStruct((count, rows, hidden), BF16),
            jax.ShapeDtypeStruct((count, rows, hidden), BF16),
        ],
        cost_estimate=cost(10 * parts),
        name="expert_pass",
    )(pref, *toks, *cots, win, wout, bin_, bout)


def expert_grad_kernel(groups, by_column, place_ref, *refs):
    sources = refs[: 2 * groups]
    keep_ref, send_ref, bias_ref = refs[2 * groups : 2 * groups + 3]
    bufs = refs[2 * groups + 3 : 4 * groups + 3]
    out_buf, load_sem, save_sem = refs[4 * groups + 3 :]
    depth = bufs[0].shape[0]
    count = sources[0].shape[0]
    cuts = out_buf.shape[1]
    half = cuts // 2

    def fetch(e, slot):
        return [
            pltpu.make_async_copy(s.at[e], b.at[slot], load_sem.at[i, slot])
            for i, (s, b) in enumerate(zip(sources, bufs))
        ]

    def save(e, side):
        return [
            pltpu.make_async_copy(out_buf.at[side, :half], keep_ref.at[:, e], save_sem.at[0, side]),
            pltpu.make_async_copy(out_buf.at[side, half:], send_ref.at[:, e], save_sem.at[1, side]),
        ]

    for e in range(min(depth, count)):
        for copy in fetch(e, e):
            copy.start()

    def one_expert(e, carry):
        slot = lax.rem(e, depth)
        side = lax.rem(e, 2)
        for copy in fetch(e, slot):
            copy.wait()
        left, right = (
            jnp.concatenate([bufs[i * groups + j][slot] for j in range(groups)], axis=0)
            for i in range(2)
        )
        grad = mul(left, right, TN)
        bias_ref[e] = jnp.sum(right.astype(F32), axis=0, keepdims=True)

        @pl.when(e >= 2)
        def _():
            for copy in save(e - 2, side):
                copy.wait()

        for i in range(cuts):
            if by_column:
                cut = grad.shape[1] // cuts
                piece = grad[:, i * cut : (i + 1) * cut]
            else:
                cut = grad.shape[0] // cuts
                piece = grad[i * cut : (i + 1) * cut]
            out_buf[side, place_ref[i]] = piece.astype(BF16)
        for copy in save(e, side):
            copy.start()

        @pl.when(e + depth < count)
        def _():
            for copy in fetch(e + depth, slot):
                copy.start()

        return carry

    lax.fori_loop(0, count, one_expert, 0)
    for e in range(max(0, count - 2), count):
        for copy in save(e, e % 2):
            copy.wait()


def expert_grads(deps, places, lefts, rights, by_column):
    groups = len(lefts)
    count = lefts[0].shape[0]
    cuts = places.shape[0]
    high, wide = lefts[0].shape[2], rights[0].shape[2]
    shape = (high, wide // cuts) if by_column else (high // cuts, wide)
    depth = min(3, count)
    sources = (*lefts, *rights)
    hbm = pl.BlockSpec(memory_space=pl.ANY)
    return call_after(
        deps,
        functools.partial(expert_grad_kernel, groups, by_column),
        in_specs=[pl.BlockSpec(memory_space=pltpu.SMEM)] + [hbm] * len(sources),
        out_specs=[hbm, hbm, pl.BlockSpec(memory_space=pltpu.VMEM)],
        out_shape=[
            jax.ShapeDtypeStruct((cuts // 2, count) + shape, BF16),
            jax.ShapeDtypeStruct((cuts - cuts // 2, count) + shape, BF16),
            jax.ShapeDtypeStruct((count, 1, wide), F32),
        ],
        scratch_shapes=[pltpu.VMEM((depth,) + s.shape[1:], BF16) for s in sources]
        + [
            pltpu.VMEM((2, cuts) + shape, BF16),
            pltpu.SemaphoreType.DMA((len(sources), depth)),
            pltpu.SemaphoreType.DMA((2, 2)),
        ],
        cost_estimate=cost(11),
        name="expert_grads",
    )(places, *sources)


TURNS = (0, 2, 1, 3)


def pick_row(array, index):
    return lax.dynamic_index_in_dim(array, index, 0, keepdims=False)


def choose(arrays, index):
    chosen = arrays[0]
    for i, a in enumerate(arrays[1:], 1):
        chosen = jnp.where(index == i, a, chosen)
    return chosen


def total(first, *more):
    first = first.astype(F32)
    for a in more:
        first = first + a.astype(F32)
    return first


def local(
    inputs,
    cotangent,
    routes,
    gates,
    attn_gain,
    attn_shift,
    qkv_weight,
    query_bias,
    value_bias,
    proj_weight,
    proj_bias,
    mlp_gain,
    mlp_shift,
    expert_in,
    expert_in_bias,
    expert_out,
    expert_out_bias,
):
    n_dp, n_expert, n_ctx = (lax.axis_size(a) for a in ("dp", "expert", "context"))
    z, y, c = (lax.axis_index(a) for a in ("dp", "expert", "context"))
    images, tok, width = inputs.shape
    count = expert_in.shape[0]
    hidden = expert_in.shape[2] // n_dp
    cut = hidden // n_ctx
    low, high = c & 1, c >> 1
    rows = 2 * tok

    def near(a):
        return lax.ppermute(a, "context", [(i, i ^ 1) for i in range(n_ctx)])

    def far(a):
        return lax.ppermute(a, "context", [(i, i ^ 2) for i in range(n_ctx)])

    def along(a, axis, n, by):
        return lax.ppermute(a, axis, [(i, (i + by) % n) for i in range(n)])

    def ring(a):
        return along(a, "dp", n_dp, 1)

    def xor_order(a):
        return jnp.stack([pick_row(a, c ^ m) for m in range(images)])

    gate_rows = gates[0].transpose(0, 2, 1)
    gate_high = gate_rows.astype(BF16)
    gate_low = (gate_rows - gate_high.astype(F32)).astype(BF16)
    small = jnp.concatenate(
        [routes[0].transpose(0, 2, 1).astype(BF16), gate_high, gate_low, gate_low], axis=1
    ).reshape(images, -1, width)
    small_rows = small.shape[1]
    small = jnp.pad(small, ((0, 0), (0, 16 - small_rows), (0, 0)))
    turned = xor_order(jnp.concatenate([inputs, cotangent, small], axis=1))
    blocks = jnp.stack([turned[:2], far(turned[2:])])
    across_near = near(blocks[:, 1, : 2 * tok])

    half_rows = qkv_weight.shape[0] // 2
    vectors = jnp.stack(
        [attn_gain, attn_shift, query_bias, value_bias, proj_bias, mlp_gain, mlp_shift, mlp_shift]
    )
    pack = lax.dynamic_slice_in_dim(
        jnp.concatenate([qkv_weight, proj_weight], axis=1), low * half_rows, half_rows, 0
    )
    pack = jnp.concatenate(
        [pack, jnp.pad(vectors, ((0, 8), (0, pack.shape[1] - vectors.shape[1])))], axis=0
    )
    got = [along(pack, "dp", n_dp, k) for k in range(1, n_dp)]

    small = blocks[:, :, 2 * tok : 2 * tok + small_rows].reshape(2, 2, 8, tok)
    entries = small[:, :, :TOP].astype(F32).transpose(0, 1, 3, 2).reshape(2, -1)
    table = (entries[:, :, None] == jnp.arange(EXPERTS, dtype=F32)[None, None, :]).astype(BF16)
    order = jnp.arange(entries.shape[1])
    lower = (order[:, None] > order[None, :]).astype(BF16)
    earlier = jnp.einsum("ij,bje->bie", lower, table, preferred_element_type=F32)
    slot_ids = jnp.sum(earlier * table.astype(F32), axis=2)
    slot_rows = slot_ids.astype(BF16).reshape(2, 2, tok, TOP).transpose(0, 1, 3, 2)
    meta = jnp.concatenate([small[:, :, :TOP], slot_rows, small[:, :, TOP : 3 * TOP]], axis=2)
    meta = meta.transpose(0, 2, 1, 3).reshape(2, 2, 4, rows).transpose(0, 2, 1, 3)
    meta = jnp.pad(meta.reshape(-1, width), ((0, META_ROWS - 8 * rows * 2 // width), (0, 0)))
    cots = blocks[:, :, tok : 2 * tok]
    cot_own = jnp.concatenate([cots[0, 0], cots[1, 0], cots[0, 1], cots[1, 1], meta], axis=0)

    def across(a):
        return [along(a, "expert", n_expert, -j) for j in range(1, n_expert)]

    def spread(own, first):
        parts = [[own] + across(own)]
        for k in range(1, n_dp):
            own = first if k == 1 else ring(own)
            parts.append([own] + across(own))
        return parts

    cot_parts = [[cot_own] + across(cot_own)]
    got = after(got, cot_own, across_near)
    other = near(jnp.stack(got))
    cot_ring = ring(cot_own)

    place = jnp.stack([z, low]).astype(jnp.int32)
    qkv, probs, attended, middle, sec_keep, sec_send, x_image, wqkv, wproj, vec = attn_fwd(
        cot_parts[0][1:],
        place,
        blocks[0, 0, :tok],
        blocks[1, 0, :tok],
        across_near[:, :tok],
        qkv_weight,
        proj_weight,
        vectors,
        other,
        got,
    )
    tok_own = jnp.concatenate([sec_keep, near(after([sec_send], cot_ring)[0])], axis=0)
    tok_parts = spread(tok_own, ring(tok_own))
    cot_parts += spread(cot_own, after([cot_ring], sec_keep)[0])[1:]

    bin_ = lax.dynamic_slice_in_dim(expert_in_bias, z * hidden, hidden, 1).astype(F32)[:, None, :]
    bout = expert_out_bias.astype(F32)[:, None, :]
    res_own, res_far, second_parts = [], [], []
    kept = [[], [], [], []]
    pref = jnp.stack([y * (count * CAP), z]).astype(jnp.int32)
    sums, travelling = {}, []

    def crossing(k):
        return [along(a, "expert", n_expert, j + 1) for j, a in enumerate(second_parts[k][1:])]

    def sum_step(k, *deps):
        (own,) = after([second_parts[k][0]], *deps)
        sums[k] = total(own, *crossed[k], *travelling)
        if k != 0:
            sums[k] = sums[k].astype(BF16)
            travelling[:] = [ring(sums[k])]

    size = max(1, 4 // n_expert)
    for first in range(0, n_dp, size):
        group = range(first, min(first + size, n_dp))
        coming = range(first + size, min(first + 2 * size, n_dp))
        outs = expert_pass(
            [parts[k][0] for k in coming for parts in (tok_parts, cot_parts)],
            n_expert - 1,
            pref,
            [a for k in group for a in tok_parts[k]],
            [a for k in group for a in cot_parts[k]],
            expert_in,
            expert_out,
            bin_,
            bout,
        )
        n = len(group) * n_expert
        second_parts += [outs[i : i + n_expert] for i in range(0, n, n_expert)]
        res_own += outs[n : n + len(group)]
        res_far.append(outs[n + len(group) : n + len(group) + n_expert - 1])
        for keep, out in zip(kept, outs[-4:]):
            keep.append(out)
    xs, gs, acts, pres = kept
    crossed = [crossing(k) for k in range(n_dp)]
    for k in range(1, max(2, n_dp - 2)):
        sum_step(k, pres[-1], *crossed[0])

    places = jnp.stack([(i ^ c) >> 1 | ((i ^ c) & 1) << 1 for i in range(n_ctx)]).astype(jnp.int32)

    def halve(keep, send):
        got = near(send)
        return keep[0], got, total(keep[1], got[1]).astype(keep.dtype)

    def in_chunks(a, *parts):
        ends = [a.shape[0] * sum(parts[: i + 1]) // sum(parts) for i in range(len(parts))]
        return [far(a[i:j]) for i, j in zip([0] + ends[:-1], ends) if j > i]

    out_keep, out_send, bias_out = expert_grads(
        [sums[max(1, n_dp - 3)]], places, acts, gs, False
    )
    sum_step(n_dp - 2, bias_out)
    *out_grad, out_sum = halve(out_keep, *after([out_send], sums[n_dp - 2]))
    in_keep, in_send, bias_in = expert_grads(
        [sums[n_dp - 2], out_sum], places, xs, pres, True
    )
    far_out = in_chunks(out_sum, 4, 12)
    sum_step(n_dp - 1, bias_in, far_out[0])
    *in_grad, in_sum = halve(in_keep, *after([in_send], sums[n_dp - 1]))
    sum_step(0, in_sum)
    grad_second = sums[0]
    bias_in = bias_in.reshape(count, n_ctx, cut).transpose(1, 0, 2)
    bias_in = jnp.stack([pick_row(bias_in, c ^ t) for t in TURNS])
    bias_out = jnp.broadcast_to(bias_out[None, :, 0], (n_ctx, count, width))
    biases = jnp.concatenate([bias_in, bias_out], axis=2)

    biases_send = near(biases[2:])
    biases_far = far(biases[1] + biases_send[1])

    gs_low = grad_second.astype(BF16)
    gs_near = near(gs_low[rows:])
    cot_image = jnp.concatenate([cots[:, 0], across_near[:, tok:]], axis=0).reshape(-1, width)
    ig_keep, ig_send, dw = attn_bwd(
        [in_sum, biases_send],
        gs_low[:rows],
        gs_near, cot_image, middle, attended, qkv, probs, x_image, wqkv, wproj, vec
    )

    res_far = [after(p, sums[n_dp - 1]) for p in res_far]
    res_got = [[along(a, "expert", n_expert, j + 1) for j, a in enumerate(p)] for p in res_far]
    span = res_own[0].shape[0]
    from_far = lambda k: [a[k % size * span : (k % size + 1) * span] for a in res_got[k // size]]
    res_own[1] = after([res_own[1]], dw)[0]
    res_ring = []
    for k in range(1, n_dp):
        res_ring.append(ring(total(res_own[k], *from_far(k), *res_ring[-1:]).astype(BF16)))

    dw = dw.reshape(n_dp, 2, half_rows, -1)
    beside = res_got[0]
    dw = total(
        *after([lax.dynamic_index_in_dim(dw, low, 1, keepdims=False)], *beside),
        near(lax.dynamic_index_in_dim(dw, 1 - low, 1, keepdims=False)),
    ).astype(BF16)

    def meet(a, m):
        step = 2 * (m & 1) + n_ctx * (m >> 1)
        pairs = [(i, i ^ step) for i in range(n_expert * n_ctx)]
        return lax.ppermute(a, ("expert", "context"), pairs)

    def over_dp(a):
        sent = [along(pick_row(a, (z + k) % n_dp), "dp", n_dp, k) for k in range(1, n_dp)]
        return total(pick_row(a, z), *sent).astype(BF16)

    if n_expert == 2:
        mine = 2 * y + high
        dw = dw.reshape(n_dp, 4, half_rows // 4, -1)
        side = lambda m: lax.dynamic_index_in_dim(dw, mine ^ m, 1, keepdims=False)
        met = [meet(side(m), m) for m in range(1, 4)]
        dw = total(*after([side(0)], *res_ring[:-2], *far_out[1:]), *met).astype(BF16)
        (in_first,) = after([in_sum[: count // 2]], dw)
        far_in = [far(in_first), far(in_sum[count // 2 :])]
        met_dw = dw
        dw = over_dp(dw)
        shares = after([dw], res_ring[-2], *far_in) + [meet(dw, m) for m in range(1, 4)]
        dw = jnp.concatenate([choose(shares, mine ^ q) for q in range(4)], axis=0)
    else:
        dw = dw + far(dw)
        dw = total(dw, *[along(dw, "expert", n_expert, j) for j in range(1, n_expert)])
        dw = dw.astype(BF16)
        far_in = in_chunks(after([in_sum], dw)[0], 1, 1)
        met_dw = dw
        dw = over_dp(dw)
    shares = after([dw], res_ring[-1], biases_far) + [near(dw)]
    dw = jnp.concatenate([choose(shares, low), choose(shares, 1 - low)], axis=0).astype(F32)
    dvec = dw[:, 4 * width : 4 * width + 8].T

    def from_blocks(first, second):
        return xor_order(jnp.concatenate([first, *after([far(second)], dw)], axis=0))

    ig_near = near(ig_send).reshape(2, tok, width)
    ig_keep = ig_keep.reshape(2, tok, width)
    input_grad = from_blocks(
        jnp.stack([ig_keep[0], ig_near[0]]), jnp.stack([ig_keep[1], ig_near[1]])
    ).astype(F32)

    combined = total(res_own[0], *from_far(0), *res_ring[-1:])
    mid_near = near(middle[rows:].astype(BF16))
    mid_blocks = jnp.concatenate([middle[:rows], mid_near.astype(F32)], axis=0)
    gate_sum = combined[2 * rows :].reshape(2, -1, width)[:, :TOP, :rows]
    gate_sum = gate_sum.reshape(2, TOP, 2, tok).transpose(2, 0, 1, 3)
    gate_sum = gate_sum.reshape(2, 2, 1, TOP * tok)
    gate_sum = jnp.pad(gate_sum.astype(BF16), ((0, 0), (0, 0), (0, 15), (0, width - TOP * tok)))
    combined = (combined[: 2 * rows] + mid_blocks).reshape(2, 2, tok, width)
    combined = jnp.concatenate([combined.astype(BF16), gate_sum], axis=2)
    combined = from_blocks(combined[:, 0], combined[:, 1])
    result = combined[:, :tok]
    gate_grad = combined[:, tok, : TOP * tok].astype(F32).reshape(images, TOP, tok)
    gate_grad = gate_grad.transpose(0, 2, 1)[None]

    biases = total(*after([biases[0]], dw), biases_send[0], biases_far)
    in_bias_grad = biases[:, :cut]
    share = width // (n_dp * n_ctx)
    out_bias_grad = lax.dynamic_slice_in_dim(biases[:, cut:], (z * n_ctx + c) * share, share, 1)
    out_got, in_got = after([out_grad[1], in_grad[1]], met_dw)
    out_grad = total(out_grad[0], out_got[0], jnp.concatenate(far_out, axis=0))
    in_grad = total(in_grad[0], in_got[0], jnp.concatenate(far_in, axis=0))

    return (
        result,
        input_grad,
        gate_grad,
        dvec[GAIN_ONE],
        dvec[SHIFT_ONE],
        dw[:, : 3 * width],
        dvec[QUERY_BIAS],
        dvec[VALUE_BIAS],
        dw[:, 3 * width : 4 * width],
        dvec[PROJ_BIAS],
        dvec[GAIN_TWO],
        dvec[SHIFT_TWO],
        in_grad,
        in_bias_grad,
        out_grad,
        out_bias_grad,
    )


def solution(mesh):
    return jax.shard_map(
        local,
        mesh=mesh,
        in_specs=(
            P(("dp", "expert"), "context", None),
            P(("dp", "expert"), "context", None),
            P("context", ("dp", "expert"), None, None),
            P("context", ("dp", "expert"), None, None),
            P("dp"),
            P("dp"),
            P("dp", None),
            P("dp"),
            P("dp"),
            P("dp", None),
            P("dp"),
            P("dp"),
            P("dp"),
            P("expert", None, None),
            P("expert", None),
            P("expert", None, None),
            P("expert", None),
        ),
        out_specs=(
            P(("dp", "expert"), "context", None),
            P(("dp", "expert"), "context", None),
            P("context", ("dp", "expert"), None, None),
            P("dp"),
            P("dp"),
            P("dp", None),
            P("dp"),
            P("dp"),
            P("dp", None),
            P("dp"),
            P("dp"),
            P("dp"),
            P("expert", None, ("dp", "context")),
            P("expert", ("dp", "context")),
            P("expert", ("dp", "context"), None),
            P("expert", ("dp", "context")),
        ),
        check_vma=False,
    )
```

```python
import functools
import math

import jax
import jax.numpy as jnp
from jax import lax
from jax.experimental import pallas as pl
from jax.experimental.pallas import tpu as pltpu
from jax.sharding import PartitionSpec as P

EXPERTS = 32
HEAD_DIM = 64
TOP = 2
CAP = 32

EPSILON = 1e-06
ROOT_HALF = 1.0 / math.sqrt(2.0)
INV_ROOT_TWO_PI = 1.0 / math.sqrt(2.0 * math.pi)
SCORE_SCALE = 1.0 / math.sqrt(HEAD_DIM)

F32 = jnp.float32
BF16 = jnp.bfloat16
VMEM_LIMIT = 56 * 1024 * 1024


def cost(microseconds):
    return pl.CostEstimate(flops=int(microseconds * 1e9), bytes_accessed=1, transcendentals=0)


GAIN_ONE, SHIFT_ONE, QUERY_BIAS, VALUE_BIAS, PROJ_BIAS, GAIN_TWO, SHIFT_TWO = range(7)

NN = (((1,), (0,)), ((), ()))
NT = (((1,), (1,)), ((), ()))
TN = (((0,), (0,)), ((), ()))


def mul(a, b, how=NN):
    return lax.dot_general(a, b, how, preferred_element_type=F32)


def norm_stats(values):
    average = jnp.mean(values, axis=-1, keepdims=True)
    centred = values - average
    inverse = lax.rsqrt(jnp.mean(centred * centred, axis=-1, keepdims=True) + EPSILON)
    return centred * inverse, inverse


def norm_back(scaled, inverse, gain_vec, grad_out):
    grad_scaled = grad_out * gain_vec
    mean_grad = jnp.mean(grad_scaled, axis=-1, keepdims=True)
    mean_cross = jnp.mean(grad_scaled * scaled, axis=-1, keepdims=True)
    return inverse * (grad_scaled - mean_grad - scaled * mean_cross)


def gelu_parts(values):
    spread = jnp.abs(values) * ROOT_HALF
    t = 1.0 / (1.0 + 0.3275911 * spread)
    series = t * (
        0.254829592
        + t * (-0.284496736 + t * (1.421413741 + t * (-1.453152027 + t * 1.061405429)))
    )
    bell = jnp.exp(-0.5 * values * values)
    tail = 0.5 * series * bell
    return jnp.where(values >= 0.0, 1.0 - tail, tail), bell * INV_ROOT_TWO_PI


def skipping(deps, kernel, *refs):
    kernel(*refs[deps:])


def call_after(deps, kernel, in_specs, **options):
    deps = list(deps)
    call = pl.pallas_call(
        functools.partial(skipping, len(deps), kernel),
        in_specs=[pl.BlockSpec(memory_space=pl.ANY)] * len(deps) + list(in_specs),
        compiler_params=pltpu.CompilerParams(vmem_limit_bytes=VMEM_LIMIT),
        **options,
    )
    return lambda *arrays: call(*deps, *arrays)


def after(arrays, *deps):
    token = lax.optimization_barrier((lax.create_token(), *deps))[0]
    return [lax.optimization_barrier((token, a))[1] for a in arrays]


def attn_fwd_kernel(
    n_dp, place_ref, own_ref, far_ref, near_ref, qkv_own_ref, proj_own_ref, vec_own_ref, other_ref,
    *refs,
):
    got = refs[: n_dp - 1]
    (
        qkv_ref, probs_ref, att_ref, mid_ref, keep_ref, send_ref, x_ref, wqkv_ref, wproj_ref, vec_ref,
        vec_scr,
    ) = refs[n_dp - 1 :]
    rows, width = x_ref.shape
    quarter = rows // 4
    x_ref[:quarter] = own_ref[...]
    x_ref[quarter : 2 * quarter] = far_ref[...]
    x_ref[2 * quarter : 3 * quarter] = near_ref[0]
    x_ref[3 * quarter :] = near_ref[1]
    z, low = place_ref[0], place_ref[1]
    part_rows = width // n_dp
    half_rows = part_rows // 2

    def put(at, block):
        at = pl.ds(pl.multiple_of(at, half_rows), block.shape[0])
        wqkv_ref[at] = block[:, : 3 * width]
        wproj_ref[at] = block[:, 3 * width :]

    at = pl.ds(pl.multiple_of(z * part_rows, part_rows), part_rows)
    wqkv_ref[at] = qkv_own_ref[...]
    wproj_ref[at] = proj_own_ref[...]
    vec_scr[z] = vec_own_ref[...].astype(F32)
    for k in range(1, n_dp):
        source = lax.rem(z + n_dp - k, n_dp)
        put(source * part_rows + low * half_rows, got[k - 1][:half_rows])
        put(source * part_rows + (1 - low) * half_rows, other_ref[k - 1, :half_rows])
        vec_scr[source] = got[k - 1][half_rows : half_rows + 16, :part_rows].astype(F32)[:8]
    vec_ref[...] = jnp.concatenate([vec_scr[k] for k in range(n_dp)], axis=1)
    pairs = width // (2 * HEAD_DIM)
    x = x_ref[...].astype(F32)
    scaled, _ = norm_stats(x)
    vec = vec_ref[...]
    normed = (scaled * vec[GAIN_ONE : GAIN_ONE + 1] + vec[SHIFT_ONE : SHIFT_ONE + 1]).astype(BF16)
    queries = mul(normed, wqkv_ref[:, :width]) + vec[QUERY_BIAS : QUERY_BIAS + 1]
    qkv_ref[:, :width] = (queries.astype(BF16).astype(F32) * SCORE_SCALE).astype(BF16)
    qkv_ref[:, width : 2 * width] = mul(normed, wqkv_ref[:, width : 2 * width]).astype(BF16)
    qkv_ref[:, 2 * width :] = (
        mul(normed, wqkv_ref[:, 2 * width :]) + vec[VALUE_BIAS : VALUE_BIAS + 1]
    ).astype(BF16)
    head_rows = lax.broadcasted_iota(jnp.int32, (2 * HEAD_DIM, 1), 0)
    for pair in range(pairs):
        at = pair * 2 * HEAD_DIM
        query_t = qkv_ref[:, at : at + 2 * HEAD_DIM].astype(F32).T
        keys = qkv_ref[:, width + at : width + at + 2 * HEAD_DIM]
        value_t = qkv_ref[:, 2 * width + at : 2 * width + at + 2 * HEAD_DIM].astype(F32).T.astype(BF16)
        outs = []
        for half in range(2):
            own = (head_rows // HEAD_DIM) == half
            scores = mul(keys, jnp.where(own, query_t, 0.0).astype(BF16))
            highest = jnp.max(scores, axis=0, keepdims=True)
            exponent = jnp.exp(scores - highest)
            total = jnp.sum(exponent, axis=0, keepdims=True)
            probs = (exponent * (1.0 / total)).astype(BF16)
            probs_ref[2 * pair + half] = probs
            outs.append(mul(value_t[half * HEAD_DIM : (half + 1) * HEAD_DIM], probs))
        att_ref[:, at : at + 2 * HEAD_DIM] = jnp.concatenate(outs, axis=0).T.astype(BF16)
    middle = x + mul(att_ref[...], wproj_ref[...]) + vec[PROJ_BIAS : PROJ_BIAS + 1]
    mid_ref[...] = middle
    scaled_two, _ = norm_stats(middle)
    second = (
        scaled_two * vec[GAIN_TWO : GAIN_TWO + 1] + vec[SHIFT_TWO : SHIFT_TWO + 1]
    ).astype(BF16)
    keep_ref[...] = second[: rows // 2]
    send_ref[...] = second[rows // 2 :]


def attn_fwd(deps, place, own, far, near, qkv_own, proj_own, vec_own, other, got):
    rows, width = 4 * own.shape[0], own.shape[1]
    heads = width // HEAD_DIM
    n_dp = len(got) + 1
    vmem = pl.BlockSpec(memory_space=pltpu.VMEM)
    return call_after(
        deps,
        functools.partial(attn_fwd_kernel, n_dp),
        in_specs=[pl.BlockSpec(memory_space=pltpu.SMEM)] + [vmem] * (7 + len(got)),
        out_specs=[vmem] * 10,
        out_shape=(
            jax.ShapeDtypeStruct((rows, 3 * width), BF16),
            jax.ShapeDtypeStruct((heads, rows, rows), BF16),
            jax.ShapeDtypeStruct((rows, width), BF16),
            jax.ShapeDtypeStruct((rows, width), F32),
            jax.ShapeDtypeStruct((rows // 2, width), BF16),
            jax.ShapeDtypeStruct((rows // 2, width), BF16),
            jax.ShapeDtypeStruct((rows, width), BF16),
            jax.ShapeDtypeStruct((width, 3 * width), BF16),
            jax.ShapeDtypeStruct((width, width), BF16),
            jax.ShapeDtypeStruct((8, width), F32),
        ),
        scratch_shapes=[pltpu.VMEM((n_dp, 8, width // n_dp), F32)],
        cost_estimate=cost(11),
        name="attn_fwd",
    )(place, own, far, near, qkv_own, proj_own, vec_own, other, *got)


def attn_bwd_kernel(
    gs_keep_ref, gs_near_ref, cot_ref, mid_ref, att_ref, qkv_ref, probs_ref, x_ref, wqkv_ref, wproj_ref, vec_ref,
    ig_keep_ref, ig_send_ref, dw_ref, gj_ref, dvec_ref,
):
    width = x_ref.shape[1]
    pairs = width // (2 * HEAD_DIM)
    dvec_ref[...] = jnp.zeros_like(dvec_ref)
    vec = vec_ref[...]
    grad_second = jnp.concatenate([gs_keep_ref[...], gs_near_ref[...]], axis=0).astype(F32)
    scaled_two, inverse_two = norm_stats(mid_ref[...])
    grad_middle = cot_ref[...].astype(F32) + norm_back(
        scaled_two, inverse_two, vec[GAIN_TWO : GAIN_TWO + 1], grad_second
    )
    dvec_ref[GAIN_TWO : GAIN_TWO + 1] = jnp.sum(grad_second * scaled_two, axis=0, keepdims=True)
    dvec_ref[SHIFT_TWO : SHIFT_TWO + 1] = jnp.sum(grad_second, axis=0, keepdims=True)
    grad_branch = grad_middle.astype(BF16)
    dvec_ref[PROJ_BIAS : PROJ_BIAS + 1] = jnp.sum(grad_branch.astype(F32), axis=0, keepdims=True)
    dw_ref[:, 3 * width : 4 * width] = mul(att_ref[...], grad_branch, TN).astype(BF16)
    grad_att = mul(grad_branch, wproj_ref[...], NT).astype(BF16)
    rows = lax.broadcasted_iota(jnp.int32, (2 * HEAD_DIM, 1), 0)
    lanes = lax.broadcasted_iota(jnp.int32, (1, 2 * HEAD_DIM), 1)
    for pair in range(pairs):
        at = pair * 2 * HEAD_DIM
        grad_heads = grad_att[:, at : at + 2 * HEAD_DIM]
        grad_t = grad_heads.astype(F32).T
        queries = qkv_ref[:, at : at + 2 * HEAD_DIM]
        key_t = qkv_ref[:, width + at : width + at + 2 * HEAD_DIM].astype(F32).T.astype(BF16)
        values = qkv_ref[:, 2 * width + at : 2 * width + at + 2 * HEAD_DIM]
        query_t, key_sides, value_sides = [], [], []
        for half in range(2):
            own = (rows // HEAD_DIM) == half
            low = probs_ref[2 * pair + half]
            probs = low.astype(F32)
            grad_probs = mul(values, jnp.where(own, grad_t, 0.0).astype(BF16))
            inner = jnp.sum(probs * grad_probs, axis=0, keepdims=True)
            grad_scores = (probs * (grad_probs - inner)).astype(BF16)
            value_sides.append(mul(low, grad_heads))
            key_sides.append(mul(grad_scores, queries))
            query_t.append(mul(key_t[half * HEAD_DIM : (half + 1) * HEAD_DIM], grad_scores))
        first = lanes < HEAD_DIM
        gj_ref[:, at : at + 2 * HEAD_DIM] = (
            jnp.concatenate(query_t, axis=0).T * SCORE_SCALE
        ).astype(BF16)
        gj_ref[:, width + at : width + at + 2 * HEAD_DIM] = jnp.where(
            first, key_sides[0], key_sides[1]
        ).astype(BF16)
        gj_ref[:, 2 * width + at : 2 * width + at + 2 * HEAD_DIM] = jnp.where(
            first, value_sides[0], value_sides[1]
        ).astype(BF16)
    dvec_ref[QUERY_BIAS : QUERY_BIAS + 1] = jnp.sum(
        gj_ref[:, :width].astype(F32), axis=0, keepdims=True
    )
    dvec_ref[VALUE_BIAS : VALUE_BIAS + 1] = jnp.sum(
        gj_ref[:, 2 * width :].astype(F32), axis=0, keepdims=True
    )
    scaled_one, inverse_one = norm_stats(x_ref[...].astype(F32))
    normed = (
        scaled_one * vec[GAIN_ONE : GAIN_ONE + 1] + vec[SHIFT_ONE : SHIFT_ONE + 1]
    ).astype(BF16)
    for part in range(3):
        at = part * width
        dw_ref[:, at : at + width] = mul(normed, gj_ref[:, at : at + width], TN).astype(BF16)
    grad_normed = mul(gj_ref[...], wqkv_ref[...], NT)
    dvec_ref[GAIN_ONE : GAIN_ONE + 1] = jnp.sum(grad_normed * scaled_one, axis=0, keepdims=True)
    dvec_ref[SHIFT_ONE : SHIFT_ONE + 1] = jnp.sum(grad_normed, axis=0, keepdims=True)
    dw_ref[:, 4 * width :] = dvec_ref[...].T.astype(BF16)
    grad_input = (
        grad_middle
        + norm_back(scaled_one, inverse_one, vec[GAIN_ONE : GAIN_ONE + 1], grad_normed)
    ).astype(BF16)
    side = grad_input.shape[0] // 2
    ig_keep_ref[...] = grad_input[:side]
    ig_send_ref[...] = grad_input[side:]


def attn_bwd(deps, gs_keep, gs_near, cot, mid, att, qkv, probs, x, wqkv, wproj, vec):
    rows, width = x.shape
    vmem = pl.BlockSpec(memory_space=pltpu.VMEM)
    return call_after(
        deps,
        attn_bwd_kernel,
        in_specs=[vmem] * 11,
        out_specs=[vmem] * 3,
        out_shape=(
            jax.ShapeDtypeStruct((rows // 2, width), BF16),
            jax.ShapeDtypeStruct((rows // 2, width), BF16),
            jax.ShapeDtypeStruct((width, 4 * width + 128), BF16),
        ),
        scratch_shapes=[pltpu.VMEM((rows, 3 * width), BF16), pltpu.VMEM((128, width), F32)],
        cost_estimate=cost(14),
        name="attn_bwd",
    )(gs_keep, gs_near, cot, mid, att, qkv, probs, x, wqkv, wproj, vec)


def block_meta(cot_ref, block):
    half = cot_ref.shape[1] // 2
    at = cot_ref.shape[0] - META_ROWS
    rows = cot_ref[at : at + META_ROWS].astype(F32)[4 * block : 4 * block + 4]
    return jnp.concatenate([rows[:, :half], rows[:, half:]], axis=0)


def block_rows(ref, block):
    quarter = (ref.shape[0] - ref.shape[0] % 64) // 4
    first = ref[block * quarter : (block + 1) * quarter]
    return jnp.concatenate([first, ref[(2 + block) * quarter : (3 + block) * quarter]], axis=0)


def expert_kernel(parts, others, pref_ref, *refs):
    toks = refs[:parts]
    cots = refs[parts : 2 * parts]
    win_ref, wout_ref, bin_ref, bout_ref = refs[2 * parts : 2 * parts + 4]
    outs = refs[2 * parts + 4 :]
    seconds = outs[:parts]
    steps = parts // (others + 1)
    outs = outs[parts:]
    results = []
    for i in range(steps):
        results.append(outs[i])
        for j in range(others):
            high = outs[i].shape[0]
            results.append(outs[steps + j].at[i * high : (i + 1) * high])
    outs = outs[steps + others :]
    xo_ref, go_ref, ao_ref, po_ref = outs[:4]
    x_scr, g_scr, a_scr, p_scr, y_scr, d_scr, in_buf, out_buf, in_sem, out_sem, keep_sem = outs[4:]
    count, _, width = x_scr.shape
    slots = count * CAP
    half = toks[0].shape[0] // 4
    first_code = pref_ref[0].astype(F32)
    depth, _, hidden = in_buf.shape
    part_at = pl.ds(pl.multiple_of(pref_ref[1] * hidden, hidden), hidden)

    def fetch(e, slot):
        return (
            pltpu.make_async_copy(win_ref.at[e, :, part_at], in_buf.at[slot], in_sem.at[slot]),
            pltpu.make_async_copy(wout_ref.at[e, part_at], out_buf.at[slot], out_sem.at[slot]),
        )

    for e in range(min(depth, count)):
        for copy in fetch(e, e):
            copy.start()

    place = lax.broadcasted_iota(jnp.int32, (slots, 2 * half), 0).astype(F32)
    for part in range(parts):
        for block in range(2):
            meta = block_meta(cots[part], block)
            codes = [meta[k : k + 1] * CAP + meta[2 + k : 3 + k] - first_code for k in range(2)]
            zero = place == codes[0]
            one = place == codes[1]
            pick = jnp.where(zero | one, 1.0, 0.0).astype(BF16)
            gated = jnp.where(zero, meta[4:5], jnp.where(one, meta[5:6], 0.0)).astype(BF16)
            at = (2 * part + block) * CAP
            x_scr[:, at : at + CAP, :] = (
                mul(pick, block_rows(toks[part], block)).astype(BF16).reshape(count, CAP, width)
            )
            g_scr[:, at : at + CAP, :] = (
                mul(gated, block_rows(cots[part], block)).astype(BF16).reshape(count, CAP, width)
            )

    def keep(e, i):
        source = (x_scr, g_scr, a_scr, p_scr)[i]
        target = (xo_ref, go_ref, ao_ref, po_ref)[i]
        return pltpu.make_async_copy(source.at[e], target.at[e], keep_sem.at[i, e])

    def one_expert(e, carry):
        slot = lax.rem(e, depth)
        for copy in fetch(e, slot):
            copy.wait()
        x = x_scr[e]
        g = g_scr[e]
        pre_act = mul(x, in_buf[slot]) + bin_ref[e]
        grad_active = mul(g, out_buf[slot], NT)
        below, density = gelu_parts(pre_act)
        active = (pre_act * below).astype(BF16)
        grad_pre = (grad_active * (below + pre_act * density)).astype(BF16)
        a_scr[e] = active
        p_scr[e] = grad_pre
        bias = jnp.where(pref_ref[1] == 0, bout_ref[e], 0.0)
        y_scr[e] = (mul(active, out_buf[slot]) + bias).astype(BF16)
        d_scr[e] = mul(grad_pre, in_buf[slot], NT).astype(BF16)
        for i in range(4):
            keep(e, i).start()

        @pl.when(e + depth < count)
        def _():
            for copy in fetch(e + depth, slot):
                copy.start()

        return carry

    lax.fori_loop(0, count, one_expert, 0)

    place = lax.broadcasted_iota(jnp.int32, (2 * half, slots), 1).astype(F32)
    for part in range(parts):
        gate_sums = []
        for block in range(2):
            meta = block_meta(cots[part], block).T
            codes = [meta[:, k : k + 1] * CAP + meta[:, 2 + k : 3 + k] - first_code for k in range(2)]
            at = (2 * part + block) * CAP
            zero = jnp.where(place == codes[0], 1.0, 0.0)
            one = jnp.where(place == codes[1], 1.0, 0.0)
            produced = y_scr[:, at : at + CAP, :].reshape(slots, width)
            grads = d_scr[:, at : at + CAP, :].reshape(slots, width)
            second = mul((zero + one).astype(BF16), grads).astype(BF16)
            seconds[part][block * half : (block + 1) * half] = second[:half]
            seconds[part][(2 + block) * half : (3 + block) * half] = second[half:]
            cot = block_rows(cots[part], block).astype(F32)
            picked_zero = mul(zero.astype(BF16), produced)
            picked_one = mul(one.astype(BF16), produced)
            gates = [meta[:, 4 + k : 5 + k] + meta[:, 6 + k : 7 + k] for k in range(2)]
            combined = (picked_zero * gates[0] + picked_one * gates[1]).astype(BF16)
            results[part][block * half : (block + 1) * half] = combined[:half]
            results[part][(2 + block) * half : (3 + block) * half] = combined[half:]
            sums = [jnp.sum(p * cot, axis=1, keepdims=True) for p in (picked_zero, picked_one)]
            sums = jnp.concatenate(sums + [jnp.zeros((2 * half, 6), F32)], axis=1).T
            gate_sums.append(jnp.concatenate([sums, jnp.zeros_like(sums)], axis=1))
        results[part][4 * half :] = jnp.concatenate(gate_sums, axis=0).astype(BF16)

    def settle(e, carry):
        for i in range(4):
            keep(e, i).wait()
        return carry

    lax.fori_loop(0, count, settle, 0)


META_ROWS = 16


def expert_pass(deps, others, pref, toks, cots, win, wout, bin_, bout):
    parts = len(toks)
    count, width = win.shape[:2]
    hidden = bin_.shape[2]
    rows = parts * 2 * CAP
    steps = parts // (others + 1)
    vmem = pl.BlockSpec(memory_space=pltpu.VMEM)
    hbm = pl.BlockSpec(memory_space=pl.ANY)
    depth = min(3, count)
    return call_after(
        deps,
        functools.partial(expert_kernel, parts, others),
        in_specs=[pl.BlockSpec(memory_space=pltpu.SMEM)] + [vmem] * (2 * parts) + [hbm, hbm, vmem, vmem],
        out_specs=[vmem] * (parts + steps + others) + [hbm] * 4,
        scratch_shapes=[pltpu.VMEM((count, rows, width), BF16)] * 2
        + [pltpu.VMEM((count, rows, hidden), BF16)] * 2
        + [pltpu.VMEM((count, rows, width), BF16)] * 2
        + [
            pltpu.VMEM((depth, width, hidden), BF16),
            pltpu.VMEM((depth, hidden, width), BF16),
            pltpu.SemaphoreType.DMA((depth,)),
            pltpu.SemaphoreType.DMA((depth,)),
            pltpu.SemaphoreType.DMA((4, count)),
        ],
        out_shape=[jax.ShapeDtypeStruct(toks[0].shape, BF16)] * parts
        + [jax.ShapeDtypeStruct(cots[0].shape, BF16)] * steps
        + [jax.ShapeDtypeStruct((steps * cots[0].shape[0], width), BF16)] * others
        + [
            jax.ShapeDtypeStruct((count, rows, width), BF16),
            jax.ShapeDtypeStruct((count, rows, width), BF16),
            jax.ShapeDtypeStruct((count, rows, hidden), BF16),
            jax.ShapeDtypeStruct((count, rows, hidden), BF16),
        ],
        cost_estimate=cost(10 * parts),
        name="expert_pass",
    )(pref, *toks, *cots, win, wout, bin_, bout)


def expert_grad_kernel(groups, by_column, place_ref, *refs):
    sources = refs[: 2 * groups]
    keep_ref, send_ref, bias_ref = refs[2 * groups : 2 * groups + 3]
    bufs = refs[2 * groups + 3 : 4 * groups + 3]
    out_buf, load_sem, save_sem = refs[4 * groups + 3 :]
    depth = bufs[0].shape[0]
    count = sources[0].shape[0]
    cuts = out_buf.shape[1]
    half = cuts // 2

    def fetch(e, slot):
        return [
            pltpu.make_async_copy(s.at[e], b.at[slot], load_sem.at[i, slot])
            for i, (s, b) in enumerate(zip(sources, bufs))
        ]

    def save(e, side):
        return [
            pltpu.make_async_copy(out_buf.at[side, :half], keep_ref.at[:, e], save_sem.at[0, side]),
            pltpu.make_async_copy(out_buf.at[side, half:], send_ref.at[:, e], save_sem.at[1, side]),
        ]

    for e in range(min(depth, count)):
        for copy in fetch(e, e):
            copy.start()

    def one_expert(e, carry):
        slot = lax.rem(e, depth)
        side = lax.rem(e, 2)
        for copy in fetch(e, slot):
            copy.wait()
        left, right = (
            jnp.concatenate([bufs[i * groups + j][slot] for j in range(groups)], axis=0)
            for i in range(2)
        )
        grad = mul(left, right, TN)
        bias_ref[e] = jnp.sum(right.astype(F32), axis=0, keepdims=True)

        @pl.when(e >= 2)
        def _():
            for copy in save(e - 2, side):
                copy.wait()

        for i in range(cuts):
            if by_column:
                cut = grad.shape[1] // cuts
                piece = grad[:, i * cut : (i + 1) * cut]
            else:
                cut = grad.shape[0] // cuts
                piece = grad[i * cut : (i + 1) * cut]
            out_buf[side, place_ref[i]] = piece.astype(BF16)
        for copy in save(e, side):
            copy.start()

        @pl.when(e + depth < count)
        def _():
            for copy in fetch(e + depth, slot):
                copy.start()

        return carry

    lax.fori_loop(0, count, one_expert, 0)
    for e in range(max(0, count - 2), count):
        for copy in save(e, e % 2):
            copy.wait()


def expert_grads(deps, places, lefts, rights, by_column):
    groups = len(lefts)
    count = lefts[0].shape[0]
    cuts = places.shape[0]
    high, wide = lefts[0].shape[2], rights[0].shape[2]
    shape = (high, wide // cuts) if by_column else (high // cuts, wide)
    depth = min(3, count)
    sources = (*lefts, *rights)
    hbm = pl.BlockSpec(memory_space=pl.ANY)
    return call_after(
        deps,
        functools.partial(expert_grad_kernel, groups, by_column),
        in_specs=[pl.BlockSpec(memory_space=pltpu.SMEM)] + [hbm] * len(sources),
        out_specs=[hbm, hbm, pl.BlockSpec(memory_space=pltpu.VMEM)],
        out_shape=[
            jax.ShapeDtypeStruct((cuts // 2, count) + shape, BF16),
            jax.ShapeDtypeStruct((cuts - cuts // 2, count) + shape, BF16),
            jax.ShapeDtypeStruct((count, 1, wide), F32),
        ],
        scratch_shapes=[pltpu.VMEM((depth,) + s.shape[1:], BF16) for s in sources]
        + [
            pltpu.VMEM((2, cuts) + shape, BF16),
            pltpu.SemaphoreType.DMA((len(sources), depth)),
            pltpu.SemaphoreType.DMA((2, 2)),
        ],
        cost_estimate=cost(11),
        name="expert_grads",
    )(places, *sources)


TURNS = (0, 2, 1, 3)


def pick_row(array, index):
    return lax.dynamic_index_in_dim(array, index, 0, keepdims=False)


def choose(arrays, index):
    chosen = arrays[0]
    for i, a in enumerate(arrays[1:], 1):
        chosen = jnp.where(index == i, a, chosen)
    return chosen


def total(first, *more):
    first = first.astype(F32)
    for a in more:
        first = first + a.astype(F32)
    return first


def local(
    inputs,
    cotangent,
    routes,
    gates,
    attn_gain,
    attn_shift,
    qkv_weight,
    query_bias,
    value_bias,
    proj_weight,
    proj_bias,
    mlp_gain,
    mlp_shift,
    expert_in,
    expert_in_bias,
    expert_out,
    expert_out_bias,
):
    n_dp, n_expert, n_ctx = (lax.axis_size(a) for a in ("dp", "expert", "context"))
    z, y, c = (lax.axis_index(a) for a in ("dp", "expert", "context"))
    images, tok, width = inputs.shape
    count = expert_in.shape[0]
    hidden = expert_in.shape[2] // n_dp
    cut = hidden // n_ctx
    low, high = c & 1, c >> 1
    rows = 2 * tok

    def near(a):
        return lax.ppermute(a, "context", [(i, i ^ 1) for i in range(n_ctx)])

    def far(a):
        return lax.ppermute(a, "context", [(i, i ^ 2) for i in range(n_ctx)])

    def along(a, axis, n, by):
        return lax.ppermute(a, axis, [(i, (i + by) % n) for i in range(n)])

    def ring(a):
        return along(a, "dp", n_dp, 1)

    def xor_order(a):
        return jnp.stack([pick_row(a, c ^ m) for m in range(images)])

    gate_rows = gates[0].transpose(0, 2, 1)
    gate_high = gate_rows.astype(BF16)
    gate_low = (gate_rows - gate_high.astype(F32)).astype(BF16)
    small = jnp.concatenate(
        [routes[0].transpose(0, 2, 1).astype(BF16), gate_high, gate_low, gate_low], axis=1
    ).reshape(images, -1, width)
    small_rows = small.shape[1]
    small = jnp.pad(small, ((0, 0), (0, 16 - small_rows), (0, 0)))
    turned = xor_order(jnp.concatenate([inputs, cotangent, small], axis=1))
    blocks = jnp.stack([turned[:2], far(turned[2:])])
    across_near = near(blocks[:, 1, : 2 * tok])

    half_rows = qkv_weight.shape[0] // 2
    vectors = jnp.stack(
        [attn_gain, attn_shift, query_bias, value_bias, proj_bias, mlp_gain, mlp_shift, mlp_shift]
    )
    pack = lax.dynamic_slice_in_dim(
        jnp.concatenate([qkv_weight, proj_weight], axis=1), low * half_rows, half_rows, 0
    )
    pack = jnp.concatenate(
        [pack, jnp.pad(vectors, ((0, 8), (0, pack.shape[1] - vectors.shape[1])))], axis=0
    )
    got = [along(pack, "dp", n_dp, k) for k in range(1, n_dp)]

    small = blocks[:, :, 2 * tok : 2 * tok + small_rows].reshape(2, 2, 8, tok)
    entries = small[:, :, :TOP].astype(F32).transpose(0, 1, 3, 2).reshape(2, -1)
    table = (entries[:, :, None] == jnp.arange(EXPERTS, dtype=F32)[None, None, :]).astype(BF16)
    order = jnp.arange(entries.shape[1])
    lower = (order[:, None] > order[None, :]).astype(BF16)
    earlier = jnp.einsum("ij,bje->bie", lower, table, preferred_element_type=F32)
    slot_ids = jnp.sum(earlier * table.astype(F32), axis=2)
    slot_rows = slot_ids.astype(BF16).reshape(2, 2, tok, TOP).transpose(0, 1, 3, 2)
    meta = jnp.concatenate([small[:, :, :TOP], slot_rows, small[:, :, TOP : 3 * TOP]], axis=2)
    meta = meta.transpose(0, 2, 1, 3).reshape(2, 2, 4, rows).transpose(0, 2, 1, 3)
    meta = jnp.pad(meta.reshape(-1, width), ((0, META_ROWS - 8 * rows * 2 // width), (0, 0)))
    cots = blocks[:, :, tok : 2 * tok]
    cot_own = jnp.concatenate([cots[0, 0], cots[1, 0], cots[0, 1], cots[1, 1], meta], axis=0)

    def across(a):
        return [along(a, "expert", n_expert, -j) for j in range(1, n_expert)]

    def spread(own, first):
        parts = [[own] + across(own)]
        for k in range(1, n_dp):
            own = first if k == 1 else ring(own)
            parts.append([own] + across(own))
        return parts

    cot_parts = [[cot_own] + across(cot_own)]
    got = after(got, cot_own, across_near)
    other = near(jnp.stack(got))
    cot_ring = ring(cot_own)

    place = jnp.stack([z, low]).astype(jnp.int32)
    qkv, probs, attended, middle, sec_keep, sec_send, x_image, wqkv, wproj, vec = attn_fwd(
        [],
        place,
        blocks[0, 0, :tok],
        blocks[1, 0, :tok],
        across_near[:, :tok],
        qkv_weight,
        proj_weight,
        vectors,
        other,
        got,
    )
    tok_own = jnp.concatenate([*after([sec_keep], cot_ring), near(sec_send)], axis=0)
    tok_parts = spread(tok_own, ring(tok_own))
    cot_parts += spread(cot_own, after([cot_ring], sec_keep)[0])[1:]

    bin_ = lax.dynamic_slice_in_dim(expert_in_bias, z * hidden, hidden, 1).astype(F32)[:, None, :]
    bout = expert_out_bias.astype(F32)[:, None, :]
    res_own, res_far, second_parts = [], [], []
    kept = [[], [], [], []]
    pref = jnp.stack([y * (count * CAP), z]).astype(jnp.int32)
    sums, travelling = {}, []

    def crossing(k):
        return [along(a, "expert", n_expert, j + 1) for j, a in enumerate(second_parts[k][1:])]

    def sum_step(k, *deps):
        (own,) = after([second_parts[k][0]], *deps)
        sums[k] = total(own, *crossed[k], *travelling)
        if k != 0:
            sums[k] = sums[k].astype(BF16)
            travelling[:] = [ring(sums[k])]

    size = max(1, 4 // n_expert)
    for first in range(0, n_dp, size):
        group = range(first, min(first + size, n_dp))
        coming = range(first + size, min(first + 2 * size, n_dp))
        outs = expert_pass(
            [parts[k][0] for k in coming for parts in (tok_parts, cot_parts)],
            n_expert - 1,
            pref,
            [a for k in group for a in tok_parts[k]],
            [a for k in group for a in cot_parts[k]],
            expert_in,
            expert_out,
            bin_,
            bout,
        )
        n = len(group) * n_expert
        second_parts += [outs[i : i + n_expert] for i in range(0, n, n_expert)]
        res_own += outs[n : n + len(group)]
        res_far.append(outs[n + len(group) : n + len(group) + n_expert - 1])
        for keep, out in zip(kept, outs[-4:]):
            keep.append(out)
    xs, gs, acts, pres = kept
    crossed = [crossing(k) for k in range(n_dp)]
    for k in range(1, max(2, n_dp - 2)):
        sum_step(k, pres[-1], *crossed[0])

    places = jnp.stack([(i ^ c) >> 1 | ((i ^ c) & 1) << 1 for i in range(n_ctx)]).astype(jnp.int32)

    def halve(keep, send):
        got = near(send)
        return keep[0], got, total(keep[1], got[1]).astype(keep.dtype)

    def in_chunks(a, *parts):
        ends = [a.shape[0] * sum(parts[: i + 1]) // sum(parts) for i in range(len(parts))]
        return [far(a[i:j]) for i, j in zip([0] + ends[:-1], ends) if j > i]

    out_keep, out_send, bias_out = expert_grads(
        [sums[max(1, n_dp - 3)]], places, acts, gs, False
    )
    sum_step(n_dp - 2, bias_out)
    *out_grad, out_sum = halve(out_keep, *after([out_send], sums[n_dp - 2]))
    in_keep, in_send, bias_in = expert_grads(
        [sums[n_dp - 2], out_sum], places, xs, pres, True
    )
    far_out = in_chunks(out_sum, 4, 12)
    sum_step(n_dp - 1, bias_in, far_out[0])
    *in_grad, in_sum = halve(in_keep, *after([in_send], sums[n_dp - 1]))
    sum_step(0, in_sum)
    grad_second = sums[0]
    bias_in = bias_in.reshape(count, n_ctx, cut).transpose(1, 0, 2)
    bias_in = jnp.stack([pick_row(bias_in, c ^ t) for t in TURNS])
    bias_out = jnp.broadcast_to(bias_out[None, :, 0], (n_ctx, count, width))
    biases = jnp.concatenate([bias_in, bias_out], axis=2)

    biases_send = near(biases[2:])
    biases_far = far(biases[1] + biases_send[1])

    gs_low = grad_second.astype(BF16)
    gs_near = near(gs_low[rows:])
    cot_image = jnp.concatenate([cots[:, 0], across_near[:, tok:]], axis=0).reshape(-1, width)
    ig_keep, ig_send, dw = attn_bwd(
        [in_sum, biases_send],
        gs_low[:rows],
        gs_near, cot_image, middle, attended, qkv, probs, x_image, wqkv, wproj, vec
    )

    res_far = [after(p, *((in_sum,) if i else (sums[n_dp - 1],))) for i, p in enumerate(res_far)]
    res_got = [[along(a, "expert", n_expert, j + 1) for j, a in enumerate(p)] for p in res_far]
    res_got = [after(a, dw) for a in res_got]
    span = res_own[0].shape[0]
    from_far = lambda k: [a[k % size * span : (k % size + 1) * span] for a in res_got[k // size]]
    res_own[1] = after([res_own[1]], dw)[0]
    res_ring = []
    for k in range(1, n_dp):
        res_ring.append(ring(total(res_own[k], *from_far(k), *res_ring[-1:]).astype(BF16)))

    dw = dw.reshape(n_dp, 2, half_rows, -1)
    beside = []
    dw = total(
        *after([lax.dynamic_index_in_dim(dw, low, 1, keepdims=False)], *beside),
        near(lax.dynamic_index_in_dim(dw, 1 - low, 1, keepdims=False)),
    ).astype(BF16)

    def meet(a, m):
        step = 2 * (m & 1) + n_ctx * (m >> 1)
        pairs = [(i, i ^ step) for i in range(n_expert * n_ctx)]
        return lax.ppermute(a, ("expert", "context"), pairs)

    def over_dp(a):
        sent = [along(pick_row(a, (z + k) % n_dp), "dp", n_dp, k) for k in range(1, n_dp)]
        return total(pick_row(a, z), *sent).astype(BF16)

    if n_expert == 2:
        mine = 2 * y + high
        dw = dw.reshape(n_dp, 4, half_rows // 4, -1)
        side = lambda m: lax.dynamic_index_in_dim(dw, mine ^ m, 1, keepdims=False)
        met = [meet(side(m), m) for m in range(1, 4)]
        dw = total(*after([side(0)], *res_ring[:-2], *far_out[1:]), *met).astype(BF16)
        (in_first,) = after([in_sum[: count // 2]], dw)
        far_in = [far(in_first), far(in_sum[count // 2 :])]
        met_dw = dw
        dw = over_dp(dw)
        shares = after([dw], res_ring[-2], *far_in) + [meet(dw, m) for m in range(1, 4)]
        dw = jnp.concatenate([choose(shares, mine ^ q) for q in range(4)], axis=0)
    else:
        dw = dw + far(dw)
        dw = total(dw, *[along(dw, "expert", n_expert, j) for j in range(1, n_expert)])
        dw = dw.astype(BF16)
        far_in = in_chunks(after([in_sum], dw)[0], 1, 1)
        met_dw = dw
        dw = over_dp(dw)
    shares = after([dw], res_ring[-1], biases_far) + [near(dw)]
    dw = jnp.concatenate([choose(shares, low), choose(shares, 1 - low)], axis=0).astype(F32)
    dvec = dw[:, 4 * width : 4 * width + 8].T

    def from_blocks(first, second):
        return xor_order(jnp.concatenate([first, *after([far(second)], dw)], axis=0))

    ig_near = near(ig_send).reshape(2, tok, width)
    ig_keep = ig_keep.reshape(2, tok, width)
    input_grad = from_blocks(
        jnp.stack([ig_keep[0], ig_near[0]]), jnp.stack([ig_keep[1], ig_near[1]])
    ).astype(F32)

    combined = total(res_own[0], *from_far(0), *res_ring[-1:])
    mid_near = near(*after([middle[rows:].astype(BF16)], dw))
    mid_blocks = jnp.concatenate([middle[:rows], mid_near.astype(F32)], axis=0)
    gate_sum = combined[2 * rows :].reshape(2, -1, width)[:, :TOP, :rows]
    gate_sum = gate_sum.reshape(2, TOP, 2, tok).transpose(2, 0, 1, 3)
    gate_sum = gate_sum.reshape(2, 2, 1, TOP * tok)
    gate_sum = jnp.pad(gate_sum.astype(BF16), ((0, 0), (0, 0), (0, 15), (0, width - TOP * tok)))
    combined = (combined[: 2 * rows] + mid_blocks).reshape(2, 2, tok, width)
    combined = jnp.concatenate([combined.astype(BF16), gate_sum], axis=2)
    combined = from_blocks(combined[:, 0], combined[:, 1])
    result = combined[:, :tok]
    gate_grad = combined[:, tok, : TOP * tok].astype(F32).reshape(images, TOP, tok)
    gate_grad = gate_grad.transpose(0, 2, 1)[None]

    biases = total(*after([biases[0]], dw), biases_send[0], biases_far)
    in_bias_grad = biases[:, :cut]
    share = width // (n_dp * n_ctx)
    out_bias_grad = lax.dynamic_slice_in_dim(biases[:, cut:], (z * n_ctx + c) * share, share, 1)
    out_got, in_got = after([out_grad[1], in_grad[1]], met_dw)
    out_grad = total(out_grad[0], out_got[0], jnp.concatenate(far_out, axis=0))
    in_grad = total(in_grad[0], in_got[0], jnp.concatenate(far_in, axis=0))

    return (
        result,
        input_grad,
        gate_grad,
        dvec[GAIN_ONE],
        dvec[SHIFT_ONE],
        dw[:, : 3 * width],
        dvec[QUERY_BIAS],
        dvec[VALUE_BIAS],
        dw[:, 3 * width : 4 * width],
        dvec[PROJ_BIAS],
        dvec[GAIN_TWO],
        dvec[SHIFT_TWO],
        in_grad,
        in_bias_grad,
        out_grad,
        out_bias_grad,
    )


def solution(mesh):
    return jax.shard_map(
        local,
        mesh=mesh,
        in_specs=(
            P(("dp", "expert"), "context", None),
            P(("dp", "expert"), "context", None),
            P("context", ("dp", "expert"), None, None),
            P("context", ("dp", "expert"), None, None),
            P("dp"),
            P("dp"),
            P("dp", None),
            P("dp"),
            P("dp"),
            P("dp", None),
            P("dp"),
            P("dp"),
            P("dp"),
            P("expert", None, None),
            P("expert", None),
            P("expert", None, None),
            P("expert", None),
        ),
        out_specs=(
            P(("dp", "expert"), "context", None),
            P(("dp", "expert"), "context", None),
            P("context", ("dp", "expert"), None, None),
            P("dp"),
            P("dp"),
            P("dp", None),
            P("dp"),
            P("dp"),
            P("dp", None),
            P("dp"),
            P("dp"),
            P("dp"),
            P("expert", None, ("dp", "context")),
            P("expert", ("dp", "context")),
            P("expert", ("dp", "context"), None),
            P("expert", ("dp", "context")),
        ),
        check_vma=False,
    )
```

```python
import functools
import math

import jax
import jax.numpy as jnp
from jax import lax
from jax.experimental import pallas as pl
from jax.experimental.pallas import tpu as pltpu
from jax.sharding import PartitionSpec as P

EXPERTS = 32
HEAD_DIM = 64
TOP = 2
CAP = 32

EPSILON = 1e-06
ROOT_HALF = 1.0 / math.sqrt(2.0)
INV_ROOT_TWO_PI = 1.0 / math.sqrt(2.0 * math.pi)
SCORE_SCALE = 1.0 / math.sqrt(HEAD_DIM)

F32 = jnp.float32
BF16 = jnp.bfloat16
VMEM_LIMIT = 46 * 1024 * 1024


def cost(microseconds):
    return pl.CostEstimate(flops=int(microseconds * 1e9), bytes_accessed=1, transcendentals=0)


GAIN_ONE, SHIFT_ONE, QUERY_BIAS, VALUE_BIAS, PROJ_BIAS, GAIN_TWO, SHIFT_TWO = range(7)

NN = (((1,), (0,)), ((), ()))
NT = (((1,), (1,)), ((), ()))
TN = (((0,), (0,)), ((), ()))


def mul(a, b, how=NN):
    return lax.dot_general(a, b, how, preferred_element_type=F32)


def norm_stats(values):
    average = jnp.mean(values, axis=-1, keepdims=True)
    centred = values - average
    inverse = lax.rsqrt(jnp.mean(centred * centred, axis=-1, keepdims=True) + EPSILON)
    return centred * inverse, inverse


def norm_back(scaled, inverse, gain_vec, grad_out):
    grad_scaled = grad_out * gain_vec
    mean_grad = jnp.mean(grad_scaled, axis=-1, keepdims=True)
    mean_cross = jnp.mean(grad_scaled * scaled, axis=-1, keepdims=True)
    return inverse * (grad_scaled - mean_grad - scaled * mean_cross)


def gelu_parts(values):
    spread = jnp.abs(values) * ROOT_HALF
    t = 1.0 / (1.0 + 0.3275911 * spread)
    series = t * (
        0.254829592
        + t * (-0.284496736 + t * (1.421413741 + t * (-1.453152027 + t * 1.061405429)))
    )
    bell = jnp.exp(-0.5 * values * values)
    tail = 0.5 * series * bell
    return jnp.where(values >= 0.0, 1.0 - tail, tail), bell * INV_ROOT_TWO_PI


def skipping(deps, kernel, *refs):
    kernel(*refs[deps:])


def call_after(deps, kernel, in_specs, **options):
    deps = list(deps)
    call = pl.pallas_call(
        functools.partial(skipping, len(deps), kernel),
        in_specs=[pl.BlockSpec(memory_space=pl.ANY)] * len(deps) + list(in_specs),
        compiler_params=pltpu.CompilerParams(vmem_limit_bytes=VMEM_LIMIT),
        **options,
    )
    return lambda *arrays: call(*deps, *arrays)


def after(arrays, *deps):
    token = lax.optimization_barrier((lax.create_token(), *deps))[0]
    return [lax.optimization_barrier((token, a))[1] for a in arrays]


def attn_fwd_kernel(
    n_dp, place_ref, own_ref, far_ref, near_ref, qkv_own_ref, proj_own_ref, vec_own_ref, other_ref,
    *refs,
):
    got = refs[: n_dp - 1]
    (
        qkv_ref, probs_ref, att_ref, mid_ref, keep_ref, send_ref, x_ref, wqkv_ref, wproj_ref, vec_ref,
        vec_scr,
    ) = refs[n_dp - 1 :]
    rows, width = x_ref.shape
    quarter = rows // 4
    x_ref[:quarter] = own_ref[...]
    x_ref[quarter : 2 * quarter] = far_ref[...]
    x_ref[2 * quarter : 3 * quarter] = near_ref[0]
    x_ref[3 * quarter :] = near_ref[1]
    z, low = place_ref[0], place_ref[1]
    part_rows = width // n_dp
    half_rows = part_rows // 2

    def put(at, block):
        at = pl.ds(pl.multiple_of(at, half_rows), block.shape[0])
        wqkv_ref[at] = block[:, : 3 * width]
        wproj_ref[at] = block[:, 3 * width :]

    at = pl.ds(pl.multiple_of(z * part_rows, part_rows), part_rows)
    wqkv_ref[at] = qkv_own_ref[...]
    wproj_ref[at] = proj_own_ref[...]
    vec_scr[z] = vec_own_ref[...].astype(F32)
    for k in range(1, n_dp):
        source = lax.rem(z + n_dp - k, n_dp)
        put(source * part_rows + low * half_rows, got[k - 1][:half_rows])
        put(source * part_rows + (1 - low) * half_rows, other_ref[k - 1, :half_rows])
        vec_scr[source] = got[k - 1][half_rows : half_rows + 16, :part_rows].astype(F32)[:8]
    vec_ref[...] = jnp.concatenate([vec_scr[k] for k in range(n_dp)], axis=1)
    pairs = width // (2 * HEAD_DIM)
    x = x_ref[...].astype(F32)
    scaled, _ = norm_stats(x)
    vec = vec_ref[...]
    normed = (scaled * vec[GAIN_ONE : GAIN_ONE + 1] + vec[SHIFT_ONE : SHIFT_ONE + 1]).astype(BF16)
    queries = mul(normed, wqkv_ref[:, :width]) + vec[QUERY_BIAS : QUERY_BIAS + 1]
    qkv_ref[:, :width] = (queries.astype(BF16).astype(F32) * SCORE_SCALE).astype(BF16)
    qkv_ref[:, width : 2 * width] = mul(normed, wqkv_ref[:, width : 2 * width]).astype(BF16)
    qkv_ref[:, 2 * width :] = (
        mul(normed, wqkv_ref[:, 2 * width :]) + vec[VALUE_BIAS : VALUE_BIAS + 1]
    ).astype(BF16)
    head_rows = lax.broadcasted_iota(jnp.int32, (2 * HEAD_DIM, 1), 0)
    for pair in range(pairs):
        at = pair * 2 * HEAD_DIM
        query_t = qkv_ref[:, at : at + 2 * HEAD_DIM].astype(F32).T
        keys = qkv_ref[:, width + at : width + at + 2 * HEAD_DIM]
        value_t = qkv_ref[:, 2 * width + at : 2 * width + at + 2 * HEAD_DIM].astype(F32).T.astype(BF16)
        outs = []
        for half in range(2):
            own = (head_rows // HEAD_DIM) == half
            scores = mul(keys, jnp.where(own, query_t, 0.0).astype(BF16))
            highest = jnp.max(scores, axis=0, keepdims=True)
            exponent = jnp.exp(scores - highest)
            total = jnp.sum(exponent, axis=0, keepdims=True)
            probs = (exponent * (1.0 / total)).astype(BF16)
            probs_ref[2 * pair + half] = probs
            outs.append(mul(value_t[half * HEAD_DIM : (half + 1) * HEAD_DIM], probs))
        att_ref[:, at : at + 2 * HEAD_DIM] = jnp.concatenate(outs, axis=0).T.astype(BF16)
    middle = x + mul(att_ref[...], wproj_ref[...]) + vec[PROJ_BIAS : PROJ_BIAS + 1]
    mid_ref[...] = middle
    scaled_two, _ = norm_stats(middle)
    second = (
        scaled_two * vec[GAIN_TWO : GAIN_TWO + 1] + vec[SHIFT_TWO : SHIFT_TWO + 1]
    ).astype(BF16)
    keep_ref[...] = second[: rows // 2]
    send_ref[...] = second[rows // 2 :]


def attn_fwd(deps, place, own, far, near, qkv_own, proj_own, vec_own, other, got):
    rows, width = 4 * own.shape[0], own.shape[1]
    heads = width // HEAD_DIM
    n_dp = len(got) + 1
    vmem = pl.BlockSpec(memory_space=pltpu.VMEM)
    return call_after(
        deps,
        functools.partial(attn_fwd_kernel, n_dp),
        in_specs=[pl.BlockSpec(memory_space=pltpu.SMEM)] + [vmem] * (7 + len(got)),
        out_specs=[vmem] * 10,
        out_shape=(
            jax.ShapeDtypeStruct((rows, 3 * width), BF16),
            jax.ShapeDtypeStruct((heads, rows, rows), BF16),
            jax.ShapeDtypeStruct((rows, width), BF16),
            jax.ShapeDtypeStruct((rows, width), F32),
            jax.ShapeDtypeStruct((rows // 2, width), BF16),
            jax.ShapeDtypeStruct((rows // 2, width), BF16),
            jax.ShapeDtypeStruct((rows, width), BF16),
            jax.ShapeDtypeStruct((width, 3 * width), BF16),
            jax.ShapeDtypeStruct((width, width), BF16),
            jax.ShapeDtypeStruct((8, width), F32),
        ),
        scratch_shapes=[pltpu.VMEM((n_dp, 8, width // n_dp), F32)],
        cost_estimate=cost(11),
        name="attn_fwd",
    )(place, own, far, near, qkv_own, proj_own, vec_own, other, *got)


def attn_bwd_kernel(
    gs_keep_ref, gs_near_ref, cot_ref, mid_ref, att_ref, qkv_ref, probs_ref, x_ref, wqkv_ref, wproj_ref, vec_ref,
    ig_keep_ref, ig_send_ref, dw_ref, gj_ref, dvec_ref,
):
    width = x_ref.shape[1]
    pairs = width // (2 * HEAD_DIM)
    dvec_ref[...] = jnp.zeros_like(dvec_ref)
    vec = vec_ref[...]
    grad_second = jnp.concatenate([gs_keep_ref[...], gs_near_ref[...]], axis=0).astype(F32)
    scaled_two, inverse_two = norm_stats(mid_ref[...])
    grad_middle = cot_ref[...].astype(F32) + norm_back(
        scaled_two, inverse_two, vec[GAIN_TWO : GAIN_TWO + 1], grad_second
    )
    dvec_ref[GAIN_TWO : GAIN_TWO + 1] = jnp.sum(grad_second * scaled_two, axis=0, keepdims=True)
    dvec_ref[SHIFT_TWO : SHIFT_TWO + 1] = jnp.sum(grad_second, axis=0, keepdims=True)
    grad_branch = grad_middle.astype(BF16)
    dvec_ref[PROJ_BIAS : PROJ_BIAS + 1] = jnp.sum(grad_branch.astype(F32), axis=0, keepdims=True)
    dw_ref[:, 3 * width : 4 * width] = mul(att_ref[...], grad_branch, TN).astype(BF16)
    grad_att = mul(grad_branch, wproj_ref[...], NT).astype(BF16)
    rows = lax.broadcasted_iota(jnp.int32, (2 * HEAD_DIM, 1), 0)
    lanes = lax.broadcasted_iota(jnp.int32, (1, 2 * HEAD_DIM), 1)
    for pair in range(pairs):
        at = pair * 2 * HEAD_DIM
        grad_heads = grad_att[:, at : at + 2 * HEAD_DIM]
        grad_t = grad_heads.astype(F32).T
        queries = qkv_ref[:, at : at + 2 * HEAD_DIM]
        key_t = qkv_ref[:, width + at : width + at + 2 * HEAD_DIM].astype(F32).T.astype(BF16)
        values = qkv_ref[:, 2 * width + at : 2 * width + at + 2 * HEAD_DIM]
        query_t, key_sides, value_sides = [], [], []
        for half in range(2):
            own = (rows // HEAD_DIM) == half
            low = probs_ref[2 * pair + half]
            probs = low.astype(F32)
            grad_probs = mul(values, jnp.where(own, grad_t, 0.0).astype(BF16))
            inner = jnp.sum(probs * grad_probs, axis=0, keepdims=True)
            grad_scores = (probs * (grad_probs - inner)).astype(BF16)
            value_sides.append(mul(low, grad_heads))
            key_sides.append(mul(grad_scores, queries))
            query_t.append(mul(key_t[half * HEAD_DIM : (half + 1) * HEAD_DIM], grad_scores))
        first = lanes < HEAD_DIM
        gj_ref[:, at : at + 2 * HEAD_DIM] = (
            jnp.concatenate(query_t, axis=0).T * SCORE_SCALE
        ).astype(BF16)
        gj_ref[:, width + at : width + at + 2 * HEAD_DIM] = jnp.where(
            first, key_sides[0], key_sides[1]
        ).astype(BF16)
        gj_ref[:, 2 * width + at : 2 * width + at + 2 * HEAD_DIM] = jnp.where(
            first, value_sides[0], value_sides[1]
        ).astype(BF16)
    dvec_ref[QUERY_BIAS : QUERY_BIAS + 1] = jnp.sum(
        gj_ref[:, :width].astype(F32), axis=0, keepdims=True
    )
    dvec_ref[VALUE_BIAS : VALUE_BIAS + 1] = jnp.sum(
        gj_ref[:, 2 * width :].astype(F32), axis=0, keepdims=True
    )
    scaled_one, inverse_one = norm_stats(x_ref[...].astype(F32))
    normed = (
        scaled_one * vec[GAIN_ONE : GAIN_ONE + 1] + vec[SHIFT_ONE : SHIFT_ONE + 1]
    ).astype(BF16)
    for part in range(3):
        at = part * width
        dw_ref[:, at : at + width] = mul(normed, gj_ref[:, at : at + width], TN).astype(BF16)
    grad_normed = mul(gj_ref[...], wqkv_ref[...], NT)
    dvec_ref[GAIN_ONE : GAIN_ONE + 1] = jnp.sum(grad_normed * scaled_one, axis=0, keepdims=True)
    dvec_ref[SHIFT_ONE : SHIFT_ONE + 1] = jnp.sum(grad_normed, axis=0, keepdims=True)
    dw_ref[:, 4 * width :] = dvec_ref[...].T.astype(BF16)
    grad_input = (
        grad_middle
        + norm_back(scaled_one, inverse_one, vec[GAIN_ONE : GAIN_ONE + 1], grad_normed)
    ).astype(BF16)
    side = grad_input.shape[0] // 2
    ig_keep_ref[...] = grad_input[:side]
    ig_send_ref[...] = grad_input[side:]


def attn_bwd(deps, gs_keep, gs_near, cot, mid, att, qkv, probs, x, wqkv, wproj, vec):
    rows, width = x.shape
    vmem = pl.BlockSpec(memory_space=pltpu.VMEM)
    return call_after(
        deps,
        attn_bwd_kernel,
        in_specs=[vmem] * 11,
        out_specs=[vmem] * 3,
        out_shape=(
            jax.ShapeDtypeStruct((rows // 2, width), BF16),
            jax.ShapeDtypeStruct((rows // 2, width), BF16),
            jax.ShapeDtypeStruct((width, 4 * width + 128), BF16),
        ),
        scratch_shapes=[pltpu.VMEM((rows, 3 * width), BF16), pltpu.VMEM((128, width), F32)],
        cost_estimate=cost(14),
        name="attn_bwd",
    )(gs_keep, gs_near, cot, mid, att, qkv, probs, x, wqkv, wproj, vec)


def block_meta(cot_ref, block):
    half = cot_ref.shape[1] // 2
    at = cot_ref.shape[0] - META_ROWS
    rows = cot_ref[at : at + META_ROWS].astype(F32)[4 * block : 4 * block + 4]
    return jnp.concatenate([rows[:, :half], rows[:, half:]], axis=0)


def block_rows(ref, block):
    quarter = (ref.shape[0] - ref.shape[0] % 64) // 4
    first = ref[block * quarter : (block + 1) * quarter]
    return jnp.concatenate([first, ref[(2 + block) * quarter : (3 + block) * quarter]], axis=0)


def expert_kernel(parts, others, pref_ref, *refs):
    toks = refs[:parts]
    cots = refs[parts : 2 * parts]
    win_ref, wout_ref, bin_ref, bout_ref = refs[2 * parts : 2 * parts + 4]
    outs = refs[2 * parts + 4 :]
    seconds = outs[:parts]
    steps = parts // (others + 1)
    outs = outs[parts:]
    results = []
    for i in range(steps):
        results.append(outs[i])
        for j in range(others):
            high = outs[i].shape[0]
            results.append(outs[steps + j].at[i * high : (i + 1) * high])
    outs = outs[steps + others :]
    xo_ref, go_ref, ao_ref, po_ref = outs[:4]
    x_scr, g_scr, a_scr, p_scr, y_scr, d_scr, in_buf, out_buf, in_sem, out_sem, keep_sem = outs[4:]
    count, _, width = x_scr.shape
    slots = count * CAP
    half = toks[0].shape[0] // 4
    first_code = pref_ref[0].astype(F32)
    depth, _, hidden = in_buf.shape
    part_at = pl.ds(pl.multiple_of(pref_ref[1] * hidden, hidden), hidden)

    def fetch(e, slot):
        return (
            pltpu.make_async_copy(win_ref.at[e, :, part_at], in_buf.at[slot], in_sem.at[slot]),
            pltpu.make_async_copy(wout_ref.at[e, part_at], out_buf.at[slot], out_sem.at[slot]),
        )

    for e in range(min(depth, count)):
        for copy in fetch(e, e):
            copy.start()

    place = lax.broadcasted_iota(jnp.int32, (slots, 2 * half), 0).astype(F32)
    for part in range(parts):
        for block in range(2):
            meta = block_meta(cots[part], block)
            codes = [meta[k : k + 1] * CAP + meta[2 + k : 3 + k] - first_code for k in range(2)]
            zero = place == codes[0]
            one = place == codes[1]
            pick = jnp.where(zero | one, 1.0, 0.0).astype(BF16)
            gated = jnp.where(zero, meta[4:5], jnp.where(one, meta[5:6], 0.0)).astype(BF16)
            at = (2 * part + block) * CAP
            x_scr[:, at : at + CAP, :] = (
                mul(pick, block_rows(toks[part], block)).astype(BF16).reshape(count, CAP, width)
            )
            g_scr[:, at : at + CAP, :] = (
                mul(gated, block_rows(cots[part], block)).astype(BF16).reshape(count, CAP, width)
            )

    def keep(e, i):
        source = (x_scr, g_scr, a_scr, p_scr)[i]
        target = (xo_ref, go_ref, ao_ref, po_ref)[i]
        return pltpu.make_async_copy(source.at[e], target.at[e], keep_sem.at[i, e])

    def one_expert(e, carry):
        slot = lax.rem(e, depth)
        for copy in fetch(e, slot):
            copy.wait()
        x = x_scr[e]
        g = g_scr[e]
        pre_act = mul(x, in_buf[slot]) + bin_ref[e]
        grad_active = mul(g, out_buf[slot], NT)
        below, density = gelu_parts(pre_act)
        active = (pre_act * below).astype(BF16)
        grad_pre = (grad_active * (below + pre_act * density)).astype(BF16)
        a_scr[e] = active
        p_scr[e] = grad_pre
        bias = jnp.where(pref_ref[1] == 0, bout_ref[e], 0.0)
        y_scr[e] = (mul(active, out_buf[slot]) + bias).astype(BF16)
        d_scr[e] = mul(grad_pre, in_buf[slot], NT).astype(BF16)
        for i in range(4):
            keep(e, i).start()

        @pl.when(e + depth < count)
        def _():
            for copy in fetch(e + depth, slot):
                copy.start()

        return carry

    lax.fori_loop(0, count, one_expert, 0)

    place = lax.broadcasted_iota(jnp.int32, (2 * half, slots), 1).astype(F32)
    for part in range(parts):
        gate_sums = []
        for block in range(2):
            meta = block_meta(cots[part], block).T
            codes = [meta[:, k : k + 1] * CAP + meta[:, 2 + k : 3 + k] - first_code for k in range(2)]
            at = (2 * part + block) * CAP
            zero = jnp.where(place == codes[0], 1.0, 0.0)
            one = jnp.where(place == codes[1], 1.0, 0.0)
            produced = y_scr[:, at : at + CAP, :].reshape(slots, width)
            grads = d_scr[:, at : at + CAP, :].reshape(slots, width)
            second = mul((zero + one).astype(BF16), grads).astype(BF16)
            seconds[part][block * half : (block + 1) * half] = second[:half]
            seconds[part][(2 + block) * half : (3 + block) * half] = second[half:]
            cot = block_rows(cots[part], block).astype(F32)
            picked_zero = mul(zero.astype(BF16), produced)
            picked_one = mul(one.astype(BF16), produced)
            gates = [meta[:, 4 + k : 5 + k] + meta[:, 6 + k : 7 + k] for k in range(2)]
            combined = (picked_zero * gates[0] + picked_one * gates[1]).astype(BF16)
            results[part][block * half : (block + 1) * half] = combined[:half]
            results[part][(2 + block) * half : (3 + block) * half] = combined[half:]
            sums = [jnp.sum(p * cot, axis=1, keepdims=True) for p in (picked_zero, picked_one)]
            sums = jnp.concatenate(sums + [jnp.zeros((2 * half, 6), F32)], axis=1).T
            gate_sums.append(jnp.concatenate([sums, jnp.zeros_like(sums)], axis=1))
        results[part][4 * half :] = jnp.concatenate(gate_sums, axis=0).astype(BF16)

    def settle(e, carry):
        for i in range(4):
            keep(e, i).wait()
        return carry

    lax.fori_loop(0, count, settle, 0)


META_ROWS = 16


def expert_pass(deps, others, pref, toks, cots, win, wout, bin_, bout):
    parts = len(toks)
    count, width = win.shape[:2]
    hidden = bin_.shape[2]
    rows = parts * 2 * CAP
    steps = parts // (others + 1)
    vmem = pl.BlockSpec(memory_space=pltpu.VMEM)
    hbm = pl.BlockSpec(memory_space=pl.ANY)
    depth = min(3, count)
    return call_after(
        deps,
        functools.partial(expert_kernel, parts, others),
        in_specs=[pl.BlockSpec(memory_space=pltpu.SMEM)] + [vmem] * (2 * parts) + [hbm, hbm, vmem, vmem],
        out_specs=[vmem] * (parts + steps + others) + [hbm] * 4,
        scratch_shapes=[pltpu.VMEM((count, rows, width), BF16)] * 2
        + [pltpu.VMEM((count, rows, hidden), BF16)] * 2
        + [pltpu.VMEM((count, rows, width), BF16)] * 2
        + [
            pltpu.VMEM((depth, width, hidden), BF16),
            pltpu.VMEM((depth, hidden, width), BF16),
            pltpu.SemaphoreType.DMA((depth,)),
            pltpu.SemaphoreType.DMA((depth,)),
            pltpu.SemaphoreType.DMA((4, count)),
        ],
        out_shape=[jax.ShapeDtypeStruct(toks[0].shape, BF16)] * parts
        + [jax.ShapeDtypeStruct(cots[0].shape, BF16)] * steps
        + [jax.ShapeDtypeStruct((steps * cots[0].shape[0], width), BF16)] * others
        + [
            jax.ShapeDtypeStruct((count, rows, width), BF16),
            jax.ShapeDtypeStruct((count, rows, width), BF16),
            jax.ShapeDtypeStruct((count, rows, hidden), BF16),
            jax.ShapeDtypeStruct((count, rows, hidden), BF16),
        ],
        cost_estimate=cost(10 * parts),
        name="expert_pass",
    )(pref, *toks, *cots, win, wout, bin_, bout)


def expert_grad_kernel(groups, by_column, place_ref, *refs):
    sources = refs[: 2 * groups]
    keep_ref, send_ref, bias_ref = refs[2 * groups : 2 * groups + 3]
    bufs = refs[2 * groups + 3 : 4 * groups + 3]
    out_buf, load_sem, save_sem = refs[4 * groups + 3 :]
    depth = bufs[0].shape[0]
    count = sources[0].shape[0]
    cuts = out_buf.shape[1]
    half = cuts // 2

    def fetch(e, slot):
        return [
            pltpu.make_async_copy(s.at[e], b.at[slot], load_sem.at[i, slot])
            for i, (s, b) in enumerate(zip(sources, bufs))
        ]

    def save(e, side):
        return [
            pltpu.make_async_copy(out_buf.at[side, :half], keep_ref.at[:, e], save_sem.at[0, side]),
            pltpu.make_async_copy(out_buf.at[side, half:], send_ref.at[:, e], save_sem.at[1, side]),
        ]

    for e in range(min(depth, count)):
        for copy in fetch(e, e):
            copy.start()

    def one_expert(e, carry):
        slot = lax.rem(e, depth)
        side = lax.rem(e, 2)
        for copy in fetch(e, slot):
            copy.wait()
        left, right = (
            jnp.concatenate([bufs[i * groups + j][slot] for j in range(groups)], axis=0)
            for i in range(2)
        )
        grad = mul(left, right, TN)
        bias_ref[e] = jnp.sum(right.astype(F32), axis=0, keepdims=True)

        @pl.when(e >= 2)
        def _():
            for copy in save(e - 2, side):
                copy.wait()

        for i in range(cuts):
            if by_column:
                cut = grad.shape[1] // cuts
                piece = grad[:, i * cut : (i + 1) * cut]
            else:
                cut = grad.shape[0] // cuts
                piece = grad[i * cut : (i + 1) * cut]
            out_buf[side, place_ref[i]] = piece.astype(BF16)
        for copy in save(e, side):
            copy.start()

        @pl.when(e + depth < count)
        def _():
            for copy in fetch(e + depth, slot):
                copy.start()

        return carry

    lax.fori_loop(0, count, one_expert, 0)
    for e in range(max(0, count - 2), count):
        for copy in save(e, e % 2):
            copy.wait()


def expert_grads(deps, places, lefts, rights, by_column):
    groups = len(lefts)
    count = lefts[0].shape[0]
    cuts = places.shape[0]
    high, wide = lefts[0].shape[2], rights[0].shape[2]
    shape = (high, wide // cuts) if by_column else (high // cuts, wide)
    depth = min(3, count)
    sources = (*lefts, *rights)
    hbm = pl.BlockSpec(memory_space=pl.ANY)
    return call_after(
        deps,
        functools.partial(expert_grad_kernel, groups, by_column),
        in_specs=[pl.BlockSpec(memory_space=pltpu.SMEM)] + [hbm] * len(sources),
        out_specs=[hbm, hbm, pl.BlockSpec(memory_space=pltpu.VMEM)],
        out_shape=[
            jax.ShapeDtypeStruct((cuts // 2, count) + shape, BF16),
            jax.ShapeDtypeStruct((cuts - cuts // 2, count) + shape, BF16),
            jax.ShapeDtypeStruct((count, 1, wide), F32),
        ],
        scratch_shapes=[pltpu.VMEM((depth,) + s.shape[1:], BF16) for s in sources]
        + [
            pltpu.VMEM((2, cuts) + shape, BF16),
            pltpu.SemaphoreType.DMA((len(sources), depth)),
            pltpu.SemaphoreType.DMA((2, 2)),
        ],
        cost_estimate=cost(11),
        name="expert_grads",
    )(places, *sources)


TURNS = (0, 2, 1, 3)


def pick_row(array, index):
    return lax.dynamic_index_in_dim(array, index, 0, keepdims=False)


def choose(arrays, index):
    chosen = arrays[0]
    for i, a in enumerate(arrays[1:], 1):
        chosen = jnp.where(index == i, a, chosen)
    return chosen


def total(first, *more):
    first = first.astype(F32)
    for a in more:
        first = first + a.astype(F32)
    return first


def local(
    inputs,
    cotangent,
    routes,
    gates,
    attn_gain,
    attn_shift,
    qkv_weight,
    query_bias,
    value_bias,
    proj_weight,
    proj_bias,
    mlp_gain,
    mlp_shift,
    expert_in,
    expert_in_bias,
    expert_out,
    expert_out_bias,
):
    n_dp, n_expert, n_ctx = (lax.axis_size(a) for a in ("dp", "expert", "context"))
    z, y, c = (lax.axis_index(a) for a in ("dp", "expert", "context"))
    images, tok, width = inputs.shape
    count = expert_in.shape[0]
    hidden = expert_in.shape[2] // n_dp
    cut = hidden // n_ctx
    low, high = c & 1, c >> 1
    rows = 2 * tok

    def near(a):
        return lax.ppermute(a, "context", [(i, i ^ 1) for i in range(n_ctx)])

    def far(a):
        return lax.ppermute(a, "context", [(i, i ^ 2) for i in range(n_ctx)])

    def along(a, axis, n, by):
        return lax.ppermute(a, axis, [(i, (i + by) % n) for i in range(n)])

    def ring(a):
        return along(a, "dp", n_dp, 1)

    def xor_order(a):
        return jnp.stack([pick_row(a, c ^ m) for m in range(images)])

    gate_rows = gates[0].transpose(0, 2, 1)
    gate_high = gate_rows.astype(BF16)
    gate_low = (gate_rows - gate_high.astype(F32)).astype(BF16)
    small = jnp.concatenate(
        [routes[0].transpose(0, 2, 1).astype(BF16), gate_high, gate_low, gate_low], axis=1
    ).reshape(images, -1, width)
    small_rows = small.shape[1]
    small = jnp.pad(small, ((0, 0), (0, 16 - small_rows), (0, 0)))
    turned = xor_order(jnp.concatenate([inputs, cotangent, small], axis=1))
    blocks = jnp.stack([turned[:2], far(turned[2:])])
    across_near = near(blocks[:, 1, : 2 * tok])

    half_rows = qkv_weight.shape[0] // 2
    vectors = jnp.stack(
        [attn_gain, attn_shift, query_bias, value_bias, proj_bias, mlp_gain, mlp_shift, mlp_shift]
    )
    pack = lax.dynamic_slice_in_dim(
        jnp.concatenate([qkv_weight, proj_weight], axis=1), low * half_rows, half_rows, 0
    )
    pack = jnp.concatenate(
        [pack, jnp.pad(vectors, ((0, 8), (0, pack.shape[1] - vectors.shape[1])))], axis=0
    )
    got = [along(pack, "dp", n_dp, k) for k in range(1, n_dp)]

    small = blocks[:, :, 2 * tok : 2 * tok + small_rows].reshape(2, 2, 8, tok)
    entries = small[:, :, :TOP].astype(F32).transpose(0, 1, 3, 2).reshape(2, -1)
    table = (entries[:, :, None] == jnp.arange(EXPERTS, dtype=F32)[None, None, :]).astype(BF16)
    order = jnp.arange(entries.shape[1])
    lower = (order[:, None] > order[None, :]).astype(BF16)
    earlier = jnp.einsum("ij,bje->bie", lower, table, preferred_element_type=F32)
    slot_ids = jnp.sum(earlier * table.astype(F32), axis=2)
    slot_rows = slot_ids.astype(BF16).reshape(2, 2, tok, TOP).transpose(0, 1, 3, 2)
    meta = jnp.concatenate([small[:, :, :TOP], slot_rows, small[:, :, TOP : 3 * TOP]], axis=2)
    meta = meta.transpose(0, 2, 1, 3).reshape(2, 2, 4, rows).transpose(0, 2, 1, 3)
    meta = jnp.pad(meta.reshape(-1, width), ((0, META_ROWS - 8 * rows * 2 // width), (0, 0)))
    cots = blocks[:, :, tok : 2 * tok]
    cot_own = jnp.concatenate([cots[0, 0], cots[1, 0], cots[0, 1], cots[1, 1], meta], axis=0)

    def across(a):
        return [along(a, "expert", n_expert, -j) for j in range(1, n_expert)]

    def spread(own, first):
        parts = [[own] + across(own)]
        for k in range(1, n_dp):
            own = first if k == 1 else ring(own)
            parts.append([own] + across(own))
        return parts

    cot_parts = [[cot_own] + across(cot_own)]
    got = after(got, cot_own, across_near)
    other = near(jnp.stack(got))
    cot_ring = ring(cot_own)

    place = jnp.stack([z, low]).astype(jnp.int32)
    qkv, probs, attended, middle, sec_keep, sec_send, x_image, wqkv, wproj, vec = attn_fwd(
        [],
        place,
        blocks[0, 0, :tok],
        blocks[1, 0, :tok],
        across_near[:, :tok],
        qkv_weight,
        proj_weight,
        vectors,
        other,
        got,
    )
    tok_own = jnp.concatenate([*after([sec_keep], cot_ring), near(sec_send)], axis=0)
    tok_parts = spread(tok_own, ring(tok_own))
    cot_parts += spread(cot_own, after([cot_ring], sec_keep)[0])[1:]

    bin_ = lax.dynamic_slice_in_dim(expert_in_bias, z * hidden, hidden, 1).astype(F32)[:, None, :]
    bout = expert_out_bias.astype(F32)[:, None, :]
    res_own, res_far, second_parts = [], [], []
    kept = [[], [], [], []]
    pref = jnp.stack([y * (count * CAP), z]).astype(jnp.int32)
    sums, travelling = {}, []

    def crossing(k):
        return [along(a, "expert", n_expert, j + 1) for j, a in enumerate(second_parts[k][1:])]

    def sum_step(k, *deps):
        (own,) = after([second_parts[k][0]], *deps)
        sums[k] = total(own, *crossed[k], *travelling)
        if k != 0:
            sums[k] = sums[k].astype(BF16)
            travelling[:] = [ring(sums[k])]

    size = max(1, 4 // n_expert)
    for first in range(0, n_dp, size):
        group = range(first, min(first + size, n_dp))
        coming = range(first + size, min(first + 2 * size, n_dp))
        outs = expert_pass(
            [parts[k][0] for k in coming for parts in (tok_parts, cot_parts)],
            n_expert - 1,
            pref,
            [a for k in group for a in tok_parts[k]],
            [a for k in group for a in cot_parts[k]],
            expert_in,
            expert_out,
            bin_,
            bout,
        )
        n = len(group) * n_expert
        second_parts += [outs[i : i + n_expert] for i in range(0, n, n_expert)]
        res_own += outs[n : n + len(group)]
        res_far.append(outs[n + len(group) : n + len(group) + n_expert - 1])
        for keep, out in zip(kept, outs[-4:]):
            keep.append(out)
    xs, gs, acts, pres = kept
    crossed = [crossing(k) for k in range(n_dp)]
    for k in range(1, max(2, n_dp - 2)):
        sum_step(k, pres[-1], *crossed[0])

    places = jnp.stack([(i ^ c) >> 1 | ((i ^ c) & 1) << 1 for i in range(n_ctx)]).astype(jnp.int32)

    def halve(keep, send):
        got = near(send)
        return keep[0], got, total(keep[1], got[1]).astype(keep.dtype)

    def in_chunks(a, *parts):
        ends = [a.shape[0] * sum(parts[: i + 1]) // sum(parts) for i in range(len(parts))]
        return [far(a[i:j]) for i, j in zip([0] + ends[:-1], ends) if j > i]

    out_keep, out_send, bias_out = expert_grads(
        [sums[max(1, n_dp - 3)]], places, acts, gs, False
    )
    sum_step(n_dp - 2, bias_out)
    *out_grad, out_sum = halve(out_keep, *after([out_send], sums[n_dp - 2]))
    in_keep, in_send, bias_in = expert_grads(
        [sums[n_dp - 2], out_sum], places, xs, pres, True
    )
    far_out = in_chunks(out_sum, 4, 12)
    sum_step(n_dp - 1, bias_in, far_out[0])
    *in_grad, in_sum = halve(in_keep, *after([in_send], sums[n_dp - 1]))
    sum_step(0, in_sum)
    grad_second = sums[0]
    bias_in = bias_in.reshape(count, n_ctx, cut).transpose(1, 0, 2)
    bias_in = jnp.stack([pick_row(bias_in, c ^ t) for t in TURNS])
    bias_out = jnp.broadcast_to(bias_out[None, :, 0], (n_ctx, count, width))
    biases = jnp.concatenate([bias_in, bias_out], axis=2)

    biases_send = near(biases[2:])
    biases_far = far(biases[1] + biases_send[1])

    gs_low = grad_second.astype(BF16)
    gs_near = near(gs_low[rows:])
    cot_image = jnp.concatenate([cots[:, 0], across_near[:, tok:]], axis=0).reshape(-1, width)
    ig_keep, ig_send, dw = attn_bwd(
        [in_sum, biases_send],
        gs_low[:rows],
        gs_near, cot_image, middle, attended, qkv, probs, x_image, wqkv, wproj, vec
    )

    res_far = [after(p, *((in_sum,) if i else (sums[n_dp - 1],))) for i, p in enumerate(res_far)]
    res_got = [[along(a, "expert", n_expert, j + 1) for j, a in enumerate(p)] for p in res_far]
    res_got = [after(a, dw) for a in res_got]
    span = res_own[0].shape[0]
    from_far = lambda k: [a[k % size * span : (k % size + 1) * span] for a in res_got[k // size]]
    res_own[1] = after([res_own[1]], dw)[0]
    res_ring = []
    for k in range(1, n_dp):
        res_ring.append(ring(total(res_own[k], *from_far(k), *res_ring[-1:]).astype(BF16)))

    dw = dw.reshape(n_dp, 2, half_rows, -1)
    beside = []
    dw = total(
        *after([lax.dynamic_index_in_dim(dw, low, 1, keepdims=False)], *beside),
        near(lax.dynamic_index_in_dim(dw, 1 - low, 1, keepdims=False)),
    ).astype(BF16)

    def meet(a, m):
        step = 2 * (m & 1) + n_ctx * (m >> 1)
        pairs = [(i, i ^ step) for i in range(n_expert * n_ctx)]
        return lax.ppermute(a, ("expert", "context"), pairs)

    def over_dp(a):
        sent = [along(pick_row(a, (z + k) % n_dp), "dp", n_dp, k) for k in range(1, n_dp)]
        return total(pick_row(a, z), *sent).astype(BF16)

    halved = dw
    if n_expert == 2:
        mine = 2 * y + high
        dw = dw.reshape(n_dp, 4, half_rows // 4, -1)
        side = lambda m: lax.dynamic_index_in_dim(dw, mine ^ m, 1, keepdims=False)
        met = [meet(side(m), m) for m in range(1, 4)]
        dw = total(*after([side(0)], *res_ring[:-2], *far_out[1:]), *met).astype(BF16)
        (in_first,) = after([in_sum[: count // 2]], halved)
        far_in = [far(in_first), far(in_sum[count // 2 :])]
        met_dw = dw
        dw = over_dp(dw)
        shares = after([dw], res_ring[-2], *far_in) + [meet(dw, m) for m in range(1, 4)]
        dw = jnp.concatenate([choose(shares, mine ^ q) for q in range(4)], axis=0)
    else:
        dw = dw + far(dw)
        dw = total(dw, *[along(dw, "expert", n_expert, j) for j in range(1, n_expert)])
        dw = dw.astype(BF16)
        far_in = in_chunks(after([in_sum], dw)[0], 1, 1)
        met_dw = dw
        dw = over_dp(dw)
    shares = after([dw], res_ring[-1], biases_far) + [near(dw)]
    dw = jnp.concatenate([choose(shares, low), choose(shares, 1 - low)], axis=0).astype(F32)
    dvec = dw[:, 4 * width : 4 * width + 8].T

    def from_blocks(first, second):
        return xor_order(jnp.concatenate([first, *after([far(second)], dw)], axis=0))

    ig_near = near(ig_send).reshape(2, tok, width)
    ig_keep = ig_keep.reshape(2, tok, width)
    input_grad = from_blocks(
        jnp.stack([ig_keep[0], ig_near[0]]), jnp.stack([ig_keep[1], ig_near[1]])
    ).astype(F32)

    combined = total(res_own[0], *from_far(0), *res_ring[-1:])
    mid_near = near(*after([middle[rows:].astype(BF16)], dw))
    mid_blocks = jnp.concatenate([middle[:rows], mid_near.astype(F32)], axis=0)
    gate_sum = combined[2 * rows :].reshape(2, -1, width)[:, :TOP, :rows]
    gate_sum = gate_sum.reshape(2, TOP, 2, tok).transpose(2, 0, 1, 3)
    gate_sum = gate_sum.reshape(2, 2, 1, TOP * tok)
    gate_sum = jnp.pad(gate_sum.astype(BF16), ((0, 0), (0, 0), (0, 15), (0, width - TOP * tok)))
    combined = (combined[: 2 * rows] + mid_blocks).reshape(2, 2, tok, width)
    combined = jnp.concatenate([combined.astype(BF16), gate_sum], axis=2)
    combined = from_blocks(combined[:, 0], combined[:, 1])
    result = combined[:, :tok]
    gate_grad = combined[:, tok, : TOP * tok].astype(F32).reshape(images, TOP, tok)
    gate_grad = gate_grad.transpose(0, 2, 1)[None]

    biases = total(*after([biases[0]], dw), biases_send[0], biases_far)
    in_bias_grad = biases[:, :cut]
    share = width // (n_dp * n_ctx)
    out_bias_grad = lax.dynamic_slice_in_dim(biases[:, cut:], (z * n_ctx + c) * share, share, 1)
    out_got, in_got = after([out_grad[1], in_grad[1]], met_dw)
    out_grad = total(out_grad[0], out_got[0], jnp.concatenate(far_out, axis=0))
    in_grad = total(in_grad[0], in_got[0], jnp.concatenate(far_in, axis=0))

    return (
        result,
        input_grad,
        gate_grad,
        dvec[GAIN_ONE],
        dvec[SHIFT_ONE],
        dw[:, : 3 * width],
        dvec[QUERY_BIAS],
        dvec[VALUE_BIAS],
        dw[:, 3 * width : 4 * width],
        dvec[PROJ_BIAS],
        dvec[GAIN_TWO],
        dvec[SHIFT_TWO],
        in_grad,
        in_bias_grad,
        out_grad,
        out_bias_grad,
    )


def solution(mesh):
    return jax.shard_map(
        local,
        mesh=mesh,
        in_specs=(
            P(("dp", "expert"), "context", None),
            P(("dp", "expert"), "context", None),
            P("context", ("dp", "expert"), None, None),
            P("context", ("dp", "expert"), None, None),
            P("dp"),
            P("dp"),
            P("dp", None),
            P("dp"),
            P("dp"),
            P("dp", None),
            P("dp"),
            P("dp"),
            P("dp"),
            P("expert", None, None),
            P("expert", None),
            P("expert", None, None),
            P("expert", None),
        ),
        out_specs=(
            P(("dp", "expert"), "context", None),
            P(("dp", "expert"), "context", None),
            P("context", ("dp", "expert"), None, None),
            P("dp"),
            P("dp"),
            P("dp", None),
            P("dp"),
            P("dp"),
            P("dp", None),
            P("dp"),
            P("dp"),
            P("dp"),
            P("expert", None, ("dp", "context")),
            P("expert", ("dp", "context")),
            P("expert", ("dp", "context"), None),
            P("expert", ("dp", "context")),
        ),
        check_vma=False,
    )
```
